32 devices in a mesh: section: 2 (over x), dp: 16 (over z, y, core).
Axes of the slice: x: 2, y: 2, z: 4, core: 2. Of those that a mesh axis runs over, the one named last changes fastest.
Arguments:
- inputs: bfloat16 [64, 256, 512], P('dp'), may hold values from -6 to 6
- lengths: int32 [64], P('dp'), may hold values from 0 to 250, as said below
- cotangent: bfloat16 [64, 256, 512], P('dp'), may hold values from -6 to 6
- norm_gain: bfloat16 [2, 2, 512], P('section'), may hold values from 0.5 to 1.5
- layer_norm_biases: bfloat16 [2, 2, 512], P('section'), may hold values from -1 to 1
- w_qkv: bfloat16 [2, 512, 1536], P('section'), may hold values from -0.25 to 0.25
- w_out: bfloat16 [2, 512, 512], P('section'), may hold values from -1.5 to 1.5
- w_up: bfloat16 [2, 512, 2048], P('section'), may hold values from -0.25 to 0.25
- b_up: bfloat16 [2, 2048], P('section'), may hold values from -1 to 1
- w_down: bfloat16 [2, 2048, 512], P('section'), may hold values from -0.125 to 0.125
- b_down: bfloat16 [2, 512], P('section'), may hold values from -1 to 1
Outputs:
- outputs: bfloat16 [2, 64, 256, 512], P('section', 'dp')
- input_grads: bfloat16 [2, 64, 256, 512], P('section', 'dp')
- norm_gain_grad: float32 [2, 2, 512], P('section')
- norm_bias_grad: float32 [2, 2, 512], P('section')
- w_qkv_grad: float32 [2, 512, 1536], P('section')
- w_out_grad: float32 [2, 512, 512], P('section')
- w_up_grad: float32 [2, 512, 2048], P('section')
- b_up_grad: float32 [2, 2048], P('section')
- w_down_grad: float32 [2, 2048, 512], P('section')
- b_down_grad: float32 [2, 512], P('section')
The draws below stay inside these ranges and needn't reach their ends.
Inputs may be any that keep to these rules, and one draw needn't show every extreme that they name: `lengths`: on each index of dp, the first slots of its 4 hold items and the rest are empty with length 0; at least 2 of them hold items and on some index all do. An item has length 64, 128 or 250, and some item has length 250.
All inputs are finite; a program needn't handle non-finite values.
Results may differ from the reference program's by a relative error of at most 0.017.
Values may be sent and summed in bfloat16 or wider, within the bound.
No kernel may reach another device: no remote copies, remote signals or barrier semaphores. Data moves between devices by JAX's collectives and lax.ppermute only.
A program may use at most 192 MiB of HBM per device.

```python
import math
import jax
import jax.numpy as jnp
from jax import lax

D = 512
HEADS = 8
HEAD = 64
FF = 2048
SEQ = 256
LONG = 250
MID = 128
SHORT = 64
SLOTS_DEV = 4
SLOTS = 64
N_SECTION = 2
N_DP = 16


def draw_lengths(key, part):
    key = jax.random.fold_in(key, 7)
    key_count, key_full, key_pick = jax.random.split(key, 3)
    counts = jax.random.randint(key_count, (N_DP,), SLOTS_DEV // 2, SLOTS_DEV + 1)
    full_device = jax.random.randint(key_full, (), 0, N_DP)
    counts = jnp.where(jnp.arange(N_DP) == full_device, SLOTS_DEV, counts)
    picks = jax.random.randint(key_pick, (N_DP, SLOTS_DEV), 0, 4)
    table = jnp.array([SHORT, MID, LONG, LONG], jnp.int32)
    item_lengths = table[picks]
    slot_index = jnp.arange(SLOTS_DEV)
    item_lengths = jnp.where(slot_index[None, :] < counts[:, None], item_lengths, 0)
    item_lengths = item_lengths.at[full_device, 0].set(LONG)
    return item_lengths.reshape(-1).astype(jnp.int32)


def levels(rng, dims, cuts, least, high):
    def one(dim, parts):
        draws = jax.random.uniform(jax.random.fold_in(jax.random.fold_in(rng, 6), dim), (parts,), jnp.float32, least / len(cuts), high / len(cuts))
        return jnp.repeat(jnp.exp(draws), dims[dim] // parts).reshape((-1,) + (1,) * (len(dims) - dim - 1))

    gain = one(*cuts[0])
    for cut in cuts[1:]:
        gain = gain * one(*cut)
    return gain


def scatter_about(key, shape, scale, bound, cuts=(), kind=jnp.bfloat16):
    values = jax.random.normal(key, shape, jnp.float32) * scale
    if len(cuts) > 0:
        values = levels(key, shape, cuts, -0.22, 0.18) * values
    return jnp.clip(values, min=-bound, max=bound).astype(kind)


def setup_inputs(seed: int = 0) -> dict:
    key_of = jax.random.split(jax.random.key(seed), 12)
    return {
        "inputs": scatter_about(key_of[0], (SLOTS, SEQ, D), 1.0, 6.0, ((0, 16),)),
        "lengths": draw_lengths(jax.random.fold_in(key_of[11], 71), 0),
        "cotangent": scatter_about(key_of[2], (SLOTS, SEQ, D), 1.0, 6.0, ((0, 16),)),
        "norm_gain": jnp.clip(1.0 + 0.1 * jax.random.normal(key_of[3], (N_SECTION, 2, D), jnp.float32), 0.5, 1.5).astype(jnp.bfloat16),
        "layer_norm_biases": scatter_about(key_of[4], (N_SECTION, 2, D), 0.2, 1.0, ((0, 2),)),
        "w_qkv": scatter_about(key_of[5], (N_SECTION, D, 3 * D), D ** -0.5, 0.25, ((0, 2),)),
        "w_out": scatter_about(key_of[6], (N_SECTION, D, D), (D // 32) ** -0.5, 1.5, ((0, 2),)),
        "w_up": scatter_about(key_of[7], (N_SECTION, D, FF), D ** -0.5, 0.25, ((0, 2),)),
        "b_up": scatter_about(key_of[8], (N_SECTION, FF), 0.2, 1.0, ((0, 2),)),
        "w_down": scatter_about(key_of[9], (N_SECTION, FF, D), FF ** -0.5, 0.125, ((0, 2),)),
        "b_down": scatter_about(key_of[10], (N_SECTION, D), 0.2, 1.0, ((0, 2),)),
    }


@jax.custom_vjp
def low(v):
    return lax.optimization_barrier(v.astype(jnp.bfloat16)).astype(jnp.float32)

@jax.custom_vjp
def low_back(v):
    return v

def low_keep(v):
    return (low(v), None)

def low_pass(kept, grad):
    return (grad,)

def back_keep(v):
    return (v, None)

def back_low(kept, grad):
    return (low(grad),)
low.defvjp(low_keep, low_pass)
low_back.defvjp(back_keep, back_low)

def layer_norm(stream, gain_row, bias_row):
    mean_val = lax.optimization_barrier(jnp.mean(stream, -1, keepdims=True))
    centred = stream - mean_val
    spread = lax.optimization_barrier(jnp.mean(centred * centred, -1, keepdims=True))
    return centred * lax.rsqrt(spread + 1e-05) * gain_row + bias_row

def matmul(left_operand, right_operand):
    return jnp.einsum('keq,qw->kew', left_operand, right_operand, precision=lax.Precision.HIGHEST)

def layer(stream, item_sizes, weights):
    gain_pair, bias_pair, w_qkv, w_out, w_up, b_up, w_down, b_down = weights
    slot_count = stream.shape[0]
    positions = jnp.arange(SEQ)
    key_valid = positions[None, :] < jnp.maximum(item_sizes, 1)[:, None]
    normed_first = low(layer_norm(stream, gain_pair[0], bias_pair[0]))
    packed = low_back(low(matmul(normed_first, w_qkv))).reshape(slot_count, SEQ, 3, HEADS, HEAD)
    queries = packed[:, :, 0]
    key_heads = packed[:, :, 1]
    values = packed[:, :, 2]
    scores = jnp.einsum('sqhe,skhe->shqk', queries, key_heads, precision=lax.Precision.HIGHEST)
    scores = low_back(scores * HEAD ** (-0.5))
    scores = jnp.where(key_valid[:, None, None, :], scores, -1e+30)
    row_peak = lax.optimization_barrier(jnp.max(scores, -1, keepdims=True))
    exp_scores = jnp.exp(scores - row_peak)
    soft_probs = exp_scores / lax.optimization_barrier(jnp.sum(exp_scores, -1, keepdims=True))
    mixed = jnp.einsum('shqk,skhe->sqhe', low(soft_probs), values, precision=lax.Precision.HIGHEST)
    mixed = low_back(low(mixed)).reshape(slot_count, SEQ, D)
    residual = stream + low_back(matmul(mixed, w_out))
    normed_second = low(layer_norm(residual, gain_pair[1], bias_pair[1]))
    hidden_pre = low_back(matmul(normed_second, w_up) + b_up)
    active = low(jax.nn.gelu(hidden_pre))
    return residual + low_back(matmul(active, w_down) + b_down)

def reference(inputs, lengths, cotangent, norm_gain, layer_norm_biases, w_qkv, w_out, w_up, b_up, w_down, b_down):
    parameters = tuple((entry.astype(jnp.float32) for entry in (norm_gain, layer_norm_biases, w_qkv, w_out, w_up, b_up, w_down, b_down)))
    group_width = math.gcd(SLOTS, 16)
    group_count = SLOTS // group_width
    scanned = (inputs.reshape(group_count, group_width, SEQ, D), lengths.reshape(group_count, group_width), cotangent.reshape(group_count, group_width, SEQ, D))

    def group_step(totals, item):
        stream, item_sizes, grad_out = item

        def whole(start, weights, offset):
            first_out = low_back(low(layer(start, item_sizes, tuple((entry[0] for entry in weights))))) + offset
            return (first_out, layer(first_out, item_sizes, tuple((entry[1] for entry in weights))))
        start = stream.astype(jnp.float32)
        (first_out, second_out), back_fn = jax.vjp(whole, start, parameters, jnp.zeros_like(start))
        row_live = (jnp.arange(SEQ)[None, :] < item_sizes[:, None]).astype(jnp.float32)
        grad_start, grad_params, grad_first = back_fn((jnp.zeros_like(first_out), grad_out.astype(jnp.float32) * row_live[:, :, None]))
        totals = jax.tree.map(jnp.add, totals, grad_params)
        return (totals, (first_out.astype(jnp.bfloat16), second_out.astype(jnp.bfloat16), grad_start.astype(jnp.bfloat16), grad_first.astype(jnp.bfloat16)))
    initial = jax.tree.map(jnp.zeros_like, parameters)
    totals, (firsts, seconds, grad_starts, grad_firsts) = lax.scan(group_step, initial, scanned)
    outputs = jnp.stack([firsts.reshape(SLOTS, SEQ, D), seconds.reshape(SLOTS, SEQ, D)])
    input_grads = jnp.stack([grad_starts.reshape(SLOTS, SEQ, D), grad_firsts.reshape(SLOTS, SEQ, D)])
    return (outputs, input_grads, totals[0], totals[1], totals[2], totals[3], totals[4], totals[5], totals[6], totals[7])
```

```python
import functools

import jax
import jax.numpy as jnp
from jax import lax
from jax.experimental import pallas as pl
from jax.experimental.pallas import tpu as pltpu
from jax.sharding import PartitionSpec as P

BF = jnp.bfloat16
F32 = jnp.float32
HEAD = 64
GROUP = 4
EPS = 1e-05
GELU_C = 0.7978845608028654
GELU_K = 0.044715
VMEM_LIMIT = 48 * 2**20


def dot(a, b):
    return lax.dot_general(a, b, (((1,), (0,)), ((), ())), preferred_element_type=F32)


def dot_t(a, b):
    return lax.dot_general(a, b, (((1,), (1,)), ((), ())), preferred_element_type=F32)


def t_dot(a, b):
    return lax.dot_general(a, b, (((0,), (0,)), ((), ())), preferred_element_type=F32)


def norm_parts(stream):
    mean = jnp.mean(stream, -1, keepdims=True)
    centred = stream - mean
    rstd = lax.rsqrt(jnp.mean(centred * centred, -1, keepdims=True) + EPS)
    return centred * rstd, rstd


def norm_back(hat, rstd, gain, grad):
    scaled = grad * gain
    a = jnp.mean(scaled, -1, keepdims=True)
    b = jnp.mean(scaled * hat, -1, keepdims=True)
    return rstd * (scaled - a - hat * b)


def gelu_and_slope(u):
    w = GELU_C + (GELU_C * GELU_K) * (u * u)
    half = 0.5 + 0.5 * jnp.tanh(u * w)
    a = u * half
    slope = half + (a - a * half) * (6.0 * w - 4.0 * GELU_C)
    return a.astype(BF), slope.astype(BF)


def head_masks(rows, axis):
    shape = (rows, GROUP * HEAD) if axis == 1 else (GROUP * HEAD, rows)
    lane = lax.broadcasted_iota(jnp.int32, shape, axis)
    return [(lane >= h * HEAD) & (lane < (h + 1) * HEAD) for h in range(GROUP)]


def layer_forward(x, limit, vec, s, wait):
    seq, width = x.shape
    ff = s["wup"].shape[1]
    gw = GROUP * HEAD
    hat, _ = norm_parts(x)
    n1 = (hat * vec[0:1, 0:width] + vec[0:1, width : 2 * width]).astype(BF)
    s["n1"][...] = n1
    wait("wqkv")
    s["qkv"][...] = dot(n1, s["wqkv"][...]).astype(BF)
    lane_masks = head_masks(seq, 1)
    row_masks = head_masks(seq, 0)
    key_bias = jnp.where(lax.broadcasted_iota(jnp.int32, (seq, 1), 0) < limit, 0.0, -1e30)
    for g in range(width // gw):
        q = s["qkv"][:, g * gw : (g + 1) * gw] * BF(HEAD**-0.5)
        k = s["qkv"][:, width + g * gw : width + (g + 1) * gw]
        v_t = s["qkv"][:, 2 * width + g * gw : 2 * width + (g + 1) * gw].T
        zero = jnp.zeros_like(q)
        mixed = jnp.zeros((gw, seq), F32)
        for h in range(GROUP):
            scores = dot_t(k, jnp.where(lane_masks[h], q, zero)) + key_bias
            e = jnp.exp(scores - jnp.max(scores, 0, keepdims=True))
            p = (e * (1.0 / jnp.sum(e, 0, keepdims=True))).astype(BF)
            s["pt"][g, :, h * seq : (h + 1) * seq] = p
            mixed = jnp.where(row_masks[h], dot(v_t, p), mixed)
        s["o"][:, g * gw : (g + 1) * gw] = mixed.T.astype(BF)
    wait("wout")
    r = x + dot(s["o"][...], s["wout"][...])
    s["r"][...] = r
    hat, _ = norm_parts(r)
    n2 = (hat * vec[0:1, 2 * width : 3 * width] + vec[0:1, 3 * width : 4 * width]).astype(BF)
    s["n2"][...] = n2
    wait("wup")
    for j in range(ff // width):
        cols = slice(j * width, (j + 1) * width)
        a, slope = gelu_and_slope(dot(n2, s["wup"][:, cols]) + vec[1:2, cols])
        s["a"][:, cols] = a
        s["d"][:, cols] = slope
    wait("wdn")
    y = s["r"][...] + vec[2:3, 0:width] + dot(s["a"][...], s["wdn"][...])
    return y.astype(BF)


def layer_backward(x, gy, vec, s, wait):
    seq, width = x.shape
    ff = s["wup"].shape[1]
    gw = GROUP * HEAD
    gyf = gy.astype(F32)
    wait("wdn")
    wait("d")
    for j in range(ff // width):
        cols = slice(j * width, (j + 1) * width)
        gu = dot_t(gy, s["wdn"][cols, :]) * s["d"][:, cols].astype(F32)
        s["gu"][:, cols] = gu.astype(BF)
    wait("wup")
    acc = dot_t(s["gu"][...], s["wup"][...])
    wait("r")
    hat, rstd = norm_parts(s["r"][...])
    s["small"][0:1, 2 * width : 3 * width] = jnp.sum(acc * hat, 0, keepdims=True)
    s["small"][0:1, 3 * width : 4 * width] = jnp.sum(acc, 0, keepdims=True)
    gr = gyf + norm_back(hat, rstd, vec[0:1, 2 * width : 3 * width], acc)
    grb = gr.astype(BF)
    s["grb"][...] = grb
    s["r"][...] = gr
    wait("wout")
    s["go"][...] = dot_t(grb, s["wout"][...]).astype(BF)
    lane_masks = head_masks(seq, 1)
    row_masks = head_masks(seq, 0)
    wait("qkv")
    wait("pt")
    for g in range(width // gw):
        q = s["qkv"][:, g * gw : (g + 1) * gw] * BF(HEAD**-0.5)
        k_t = s["qkv"][:, width + g * gw : width + (g + 1) * gw].T
        v = s["qkv"][:, 2 * width + g * gw : 2 * width + (g + 1) * gw]
        go = s["go"][:, g * gw : (g + 1) * gw]
        zero = jnp.zeros_like(q)
        gq = jnp.zeros((gw, seq), F32)
        for h in range(GROUP):
            cols = slice(h * seq, (h + 1) * seq)
            p = s["pt"][g, :, cols].astype(F32)
            go_h = jnp.where(lane_masks[h], go, zero)
            s["gos"][cols, :] = go_h
            s["qs"][cols, :] = jnp.where(lane_masks[h], q, zero)
            gp = dot_t(v, go_h)
            gs = (p * (gp - jnp.sum(gp * p, 0, keepdims=True))).astype(BF)
            s["gst"][:, cols] = gs
            gq = jnp.where(row_masks[h], dot(k_t, gs), gq)
        s["gqkv"][:, g * gw : (g + 1) * gw] = (gq.T * HEAD**-0.5).astype(BF)
        s["gqkv"][:, width + g * gw : width + (g + 1) * gw] = dot(
            s["gst"][...], s["qs"][...]
        ).astype(BF)
        s["gqkv"][:, 2 * width + g * gw : 2 * width + (g + 1) * gw] = dot(
            s["pt"][g], s["gos"][...]
        ).astype(BF)
    wait("wqkv")
    gn = dot_t(s["gqkv"][...], s["wqkv"][...])
    hat, rstd = norm_parts(x)
    s["small"][0:1, 0:width] = jnp.sum(gn * hat, 0, keepdims=True)
    s["small"][0:1, width : 2 * width] = jnp.sum(gn, 0, keepdims=True)
    return (s["r"][...] + norm_back(hat, rstd, vec[0:1, 0:width], gn)).astype(BF)


WEIGHTS = ("wqkv", "wout", "wup", "wdn")
KEPT = ("qkv", "pt", "r", "d")
FROM_FORWARD = ("n1", "n2", "o", "a")
FROM_BACKWARD = ("gu", "grb", "gqkv", "small")
STORES = KEPT + FROM_FORWARD + FROM_BACKWARD + ("outputs", "grads")


def shapes_of(seq, width, ff):
    gw = GROUP * HEAD
    return {
        "qkv": ((seq, 3 * width), BF),
        "pt": ((width // gw, seq, GROUP * seq), BF),
        "r": ((seq, width), F32),
        "d": ((seq, ff), BF),
        "n1": ((seq, width), BF),
        "n2": ((seq, width), BF),
        "o": ((seq, width), BF),
        "a": ((seq, ff), BF),
        "gu": ((seq, ff), BF),
        "grb": ((seq, width), BF),
        "gqkv": ((seq, 3 * width), BF),
        "small": ((8, 4 * width), F32),
        "outputs": ((seq, width), BF),
        "grads": ((seq, width), BF),
    }


def step_body(step, slots, names, sems_of, *refs):
    ref = dict(zip(names, refs))
    sc = ref["sc"]
    first = sc[0] == 0
    vec = ref["vec"]
    sems = ref["sems"]
    s = {k: ref["v_" + k] for k in sems_of if "v_" + k in ref}
    for k in ("go", "gst", "qs", "gos"):
        if "v_" + k in ref:
            s[k] = ref["v_" + k]

    def copy(name, src, dst):
        return pltpu.make_async_copy(src, dst, sems.at[sems_of.index(name)])

    def load_weights(order):
        for name in order:
            copy(name, ref[name], s[name]).start()

    def wait_weight(name):
        copy(name, ref[name], s[name]).wait()

    def stores(names, slot, begin):
        for name in names:
            c = copy("out_" + name, s[name], ref["h_" + name].at[slot])
            if begin:
                c.start()
            else:
                c.wait()

    def send(src, begin):
        c = copy("send", src, ref["send"])
        if begin:
            c.start()
        else:
            c.wait()

    has_recv = "recv" in ref

    if step < slots:

        @pl.when(first)
        def _():
            load_weights(WEIGHTS)
            c = copy("x", ref["inputs"].at[step], s["x"])
            c.start()
            c.wait()
            y = layer_forward(
                s["x"][...].astype(F32), jnp.maximum(sc[1 + step], 1), vec, s, wait_weight
            )
            s["outputs"][...] = y
            send(s["outputs"], True)
            stores(KEPT + FROM_FORWARD + ("outputs",), step, True)
            stores(KEPT + FROM_FORWARD + ("outputs",), step, False)
            send(s["outputs"], False)

    if has_recv and step < slots + 2:

        @pl.when(jnp.logical_not(first))
        def _():
            slot = step - 2
            load_weights(WEIGHTS)
            cx = copy("x", ref["recv"], s["x"])
            cx.start()
            cg = copy("gy", ref["cotangent"].at[slot], s["gy"])
            cg.start()
            cx.wait()
            length = sc[1 + slot]
            x = s["x"][...].astype(F32)
            s["outputs"][...] = layer_forward(x, jnp.maximum(length, 1), vec, s, wait_weight)
            stores(FROM_FORWARD + ("outputs",), slot, True)
            cg.wait()
            gy = s["gy"][...]
            live = lax.broadcasted_iota(jnp.int32, gy.shape, 0) < length
            gy = jnp.where(live, gy, jnp.zeros_like(gy))
            x = s["x"][...].astype(F32)
            s["grads"][...] = layer_backward(x, gy, vec, s, lambda name: None)
            send(s["grads"], True)
            stores(FROM_BACKWARD + ("grads",), slot, True)
            stores(FROM_FORWARD + FROM_BACKWARD + ("outputs", "grads"), slot, False)
            send(s["grads"], False)

    if has_recv and step >= slots:

        @pl.when(first)
        def _():
            slot = step - slots

            def kept(name):
                return copy(name, ref["h_" + name].at[slot], s[name])

            cg = copy("gy", ref["recv"], s["gy"])
            cg.start()
            load_weights(("wdn",))
            kept("d").start()
            load_weights(("wup",))
            kept("r").start()
            load_weights(("wout",))
            kept("qkv").start()
            kept("pt").start()
            load_weights(("wqkv",))
            cx = copy("x", ref["inputs"].at[slot], s["x"])
            cx.start()
            cg.wait()
            cx.wait()

            def wait(name):
                if name in WEIGHTS:
                    wait_weight(name)
                else:
                    kept(name).wait()

            s["grads"][...] = layer_backward(
                s["x"][...].astype(F32), s["gy"][...], vec, s, wait
            )
            stores(FROM_BACKWARD + ("grads",), slot, True)
            stores(FROM_BACKWARD + ("grads",), slot, False)


def pipeline_step(step, sc, vec, weights, inputs, cotangent, recv, held):
    slots, seq, width = inputs.shape
    ff = weights["wup"].shape[1]
    shapes = shapes_of(seq, width, ff)
    any_spec = pl.BlockSpec(memory_space=pl.ANY)
    names, args, specs = [], [], []

    def give(name, value, spec):
        names.append(name)
        args.append(value)
        specs.append(spec)

    give("sc", sc, pl.BlockSpec(memory_space=pltpu.SMEM))
    give("vec", vec, pl.BlockSpec(memory_space=pltpu.VMEM))
    for name in WEIGHTS:
        give(name, weights[name], any_spec)
    give("inputs", inputs, any_spec)
    give("cotangent", cotangent, any_spec)
    if recv is not None:
        give("recv", recv, any_spec)
    aliases = {}
    if held is not None:
        for i, name in enumerate(STORES):
            aliases[len(args)] = i
            give("in_" + name, held[name], any_spec)
    out_shape = [jax.ShapeDtypeStruct((slots,) + shapes[n][0], shapes[n][1]) for n in STORES]
    out_names = ["h_" + n for n in STORES]
    sends = step < slots + 2
    if sends:
        out_shape.append(jax.ShapeDtypeStruct((seq, width), BF))
        out_names.append("send")
    gw = GROUP * HEAD
    scratch = {k: v for k, v in shapes.items()}
    scratch["x"] = ((seq, width), BF)
    scratch["gy"] = ((seq, width), BF)
    scratch["go"] = ((seq, width), BF)
    scratch["gst"] = ((seq, GROUP * seq), BF)
    scratch["qs"] = ((GROUP * seq, gw), BF)
    scratch["gos"] = ((GROUP * seq, gw), BF)
    for name in WEIGHTS:
        scratch[name] = (weights[name].shape, BF)
    sems_of = list(WEIGHTS) + ["x", "gy"] + list(STORES) + ["out_" + n for n in STORES] + ["send"]
    all_names = (
        names + out_names + ["v_" + k for k in scratch] + ["sems"]
    )
    rows = seq * 3 * 2 * (width * 4 * width + 2 * width * ff)
    out = pl.pallas_call(
        functools.partial(step_body, step, slots, all_names, sems_of),
        in_specs=specs,
        out_specs=[any_spec] * len(out_shape),
        out_shape=out_shape,
        scratch_shapes=[pltpu.VMEM(shape, kind) for shape, kind in scratch.values()]
        + [pltpu.SemaphoreType.DMA((len(sems_of),))],
        input_output_aliases=aliases,
        compiler_params=pltpu.CompilerParams(vmem_limit_bytes=VMEM_LIMIT),
        cost_estimate=pl.CostEstimate(flops=rows, bytes_accessed=8 * 2**20, transcendentals=0),
        name=f"step_{step}",
    )(*args)
    held = dict(zip(STORES, out))
    return held, (out[len(STORES)] if sends else None)


def place_block(keep, send, position, block_row, value):
    rows = value.shape[0] // 4
    value = value.astype(BF)
    for place in range(4):
        ref = (keep, send)[place // 2]
        quarter = lax.bitwise_xor(place, position)
        for q in range(4):

            @pl.when(quarter == q)
            def _(q=q, ref=ref, place=place):
                ref[place % 2, block_row : block_row + rows, :] = value[q * rows : (q + 1) * rows, :]


def down_body(first_col, cols, slots, sc, recvs, cot, a_hbm, keep, send, gm, av, sems):
    width = gm.shape[-1]
    seq = gm.shape[1]
    ca = pltpu.make_async_copy(a_hbm.at[:, :, pl.ds(first_col, cols)], av, sems.at[slots])
    ca.start()

    @pl.when(sc[0] == 0)
    def _():
        for k in range(slots):
            pltpu.make_async_copy(recvs[k], gm.at[k], sems.at[k]).start()

    @pl.when(sc[0] != 0)
    def _():
        for k in range(slots):
            pltpu.make_async_copy(cot.at[k], gm.at[k], sems.at[k]).start()

    for k in range(slots):
        pltpu.make_async_copy(cot.at[k], gm.at[k], sems.at[k]).wait()
        live = lax.broadcasted_iota(jnp.int32, (seq, width), 0) < jnp.where(
            sc[0] == 0, seq, sc[1 + k]
        )
        gm[k] = jnp.where(live, gm[k], jnp.zeros((seq, width), BF))
    ca.wait()
    g = gm[...].reshape(slots * seq, width)
    for b in range(cols // width):
        left = av[:, :, b * width : (b + 1) * width].reshape(slots * seq, width)
        place_block(keep, send, sc[1 + slots], b * (width // 4), t_dot(left, g))


def down_gradient(first_col, cols, sc, recvs, cotangent, a):
    slots, seq, width = cotangent.shape
    any_spec = pl.BlockSpec(memory_space=pl.ANY)
    n = len(recvs)

    def body(sc_ref, *refs):
        recv_refs = refs[:n]
        down_body(first_col, cols, slots, sc_ref, recv_refs, *refs[n:])

    out = jax.ShapeDtypeStruct((2, cols // 4, width), BF)
    return pl.pallas_call(
        body,
        in_specs=[pl.BlockSpec(memory_space=pltpu.SMEM)] + [any_spec] * (n + 2),
        out_specs=[pl.BlockSpec(memory_space=pltpu.VMEM)] * 2,
        out_shape=[out, out],
        scratch_shapes=[
            pltpu.VMEM((slots, seq, width), BF),
            pltpu.VMEM((slots, seq, cols), BF),
            pltpu.SemaphoreType.DMA((slots + 1,)),
        ],
        compiler_params=pltpu.CompilerParams(vmem_limit_bytes=VMEM_LIMIT),
        cost_estimate=pl.CostEstimate(
            flops=2 * slots * seq * width * cols, bytes_accessed=4 * 2**20, transcendentals=0
        ),
        name=f"w_down_grad_{first_col}",
    )(sc, *recvs, cotangent, a)


def product_body(jobs, slots, with_small, sc, *refs):
    n_src = 1 + max(max(i, j) for i, j, _ in jobs)
    srcs = refs[:n_src]
    rest = refs[n_src:]
    if with_small:
        small, gu, recvs_gm = rest[0], rest[1], None
        rest = rest[2:]
    keep, send, left_v, right_v, sems = rest[:5]
    width = left_v.shape[-1]
    seq = left_v.shape[2]
    lefts = []
    for i, _, _ in jobs:
        if i not in lefts:
            lefts.append(i)
    lcopies = [
        pltpu.make_async_copy(srcs[i], left_v.at[n], sems.at[n]) for n, i in enumerate(lefts)
    ]
    rcopies = [
        pltpu.make_async_copy(
            srcs[j].at[:, :, pl.ds(c, width)], right_v.at[n], sems.at[len(lefts) + n]
        )
        for n, (_, j, c) in enumerate(jobs)
    ]
    lcopies[0].start()
    for c in rcopies[:1] + lcopies[1:] + rcopies[1:]:
        c.start()
    waited = set()
    for n, (i, _, _) in enumerate(jobs):
        at = lefts.index(i)
        if at not in waited:
            waited.add(at)
            lcopies[at].wait()
        rcopies[n].wait()
        left = left_v[at].reshape(slots * seq, width)
        right = right_v[n].reshape(slots * seq, width)
        place_block(keep, send, sc[1 + slots], n * (width // 4), t_dot(left, right))


def products(jobs, sc, sources, name):
    slots, seq, width = sources[0].shape
    any_spec = pl.BlockSpec(memory_space=pl.ANY)
    n_left = len({i for i, _, _ in jobs})
    out = jax.ShapeDtypeStruct((2, len(jobs) * width // 4, width), BF)
    return pl.pallas_call(
        functools.partial(product_body, jobs, slots, False),
        in_specs=[pl.BlockSpec(memory_space=pltpu.SMEM)] + [any_spec] * len(sources),
        out_specs=[pl.BlockSpec(memory_space=pltpu.VMEM)] * 2,
        out_shape=[out, out],
        scratch_shapes=[
            pltpu.VMEM((n_left, slots, seq, width), BF),
            pltpu.VMEM((len(jobs), slots, seq, width), BF),
            pltpu.SemaphoreType.DMA((n_left + len(jobs),)),
        ],
        compiler_params=pltpu.CompilerParams(vmem_limit_bytes=VMEM_LIMIT),
        cost_estimate=pl.CostEstimate(
            flops=2 * slots * seq * width * width * len(jobs),
            bytes_accessed=4 * 2**20,
            transcendentals=0,
        ),
        name=name,
    )(sc, *sources)


def add_rounded(a, b):
    return (a.astype(F32) + b.astype(F32)).astype(BF)


def sum_over_dp(keep, send):
    n = lax.axis_size("dp")
    me = lax.axis_index("dp")

    def exchange(value, fn):
        return lax.ppermute(value, "dp", [(i, fn(i)) for i in range(n)])

    both = add_rounded(keep, exchange(send, lambda i: i ^ 1))
    mine = add_rounded(both[0], exchange(both[1], lambda i: i ^ 2))
    if n == 16:
        z = me // 4
        outer = (z == 0) | (z == 3)

        def middle(i):
            return {1: i + 4, 2: i - 4}.get(i // 4, i)

        part = add_rounded(mine, exchange(mine, lambda i: i ^ 4))
        part = add_rounded(part, exchange(part, middle))
        back = exchange(part, lambda i: i ^ 4)
        mine = jnp.where(outer, back, part)
    else:
        bit = 4
        while bit < n:
            mine = add_rounded(mine, exchange(mine, lambda i, bit=bit: i ^ bit))
            bit *= 2
    near = jnp.stack([mine, exchange(mine, lambda i: i ^ 2)])
    far = exchange(near, lambda i: i ^ 1)
    return near, far


def unpack_body(plan, sc_at, n_parts, sc, *refs):
    parts = refs[:n_parts]
    outs = refs[n_parts:]
    position = sc[sc_at]
    for part, row, rows, out, out_row, col in plan:
        width = parts[part].shape[-1]
        for place in range(2):
            quarter = lax.bitwise_xor(position, place + 2 * (part % 2))
            at = pl.multiple_of(out_row + quarter * rows, rows)
            outs[out][pl.ds(at, rows), col : col + width] = parts[part][
                place, row : row + rows, :
            ].astype(F32)


def unpack(plan, sc, sc_at, parts, out_shapes, name):
    vmem = pl.BlockSpec(memory_space=pltpu.VMEM)
    return pl.pallas_call(
        functools.partial(unpack_body, plan, sc_at, len(parts)),
        in_specs=[pl.BlockSpec(memory_space=pltpu.SMEM)] + [vmem] * len(parts),
        out_specs=[vmem] * len(out_shapes),
        out_shape=[jax.ShapeDtypeStruct(shape, F32) for shape in out_shapes],
        compiler_params=pltpu.CompilerParams(vmem_limit_bytes=VMEM_LIMIT),
        name=name,
    )(sc, *parts)


def per_device(
    inputs,
    lengths,
    cotangent,
    norm_gain,
    layer_norm_biases,
    w_qkv,
    w_out,
    w_up,
    b_up,
    w_down,
    b_down,
):
    slots, seq, width = inputs.shape
    ff = w_up.shape[-1]
    blocks = ff // width
    section = lax.axis_index("section")
    position = lax.axis_index("dp")
    position = (position % 2) * 2 + (position // 2) % 2
    sc = jnp.concatenate(
        [
            section[None].astype(jnp.int32),
            lengths.astype(jnp.int32),
            position[None].astype(jnp.int32),
        ]
    )
    weights = {"wqkv": w_qkv[0], "wout": w_out[0], "wup": w_up[0], "wdn": w_down[0]}
    vec = jnp.zeros((8, ff), F32)
    norms = jnp.stack([norm_gain[0], layer_norm_biases[0]], 1).astype(F32).reshape(1, -1)
    vec = vec.at[0:1].set(norms)
    vec = vec.at[1:2].set(b_up.astype(F32))
    vec = vec.at[2:3, :width].set(b_down.astype(F32))

    held, recvs = None, {}
    for step in range(2 * slots):
        held, out = pipeline_step(
            step, sc, vec, weights, inputs, cotangent, recvs.get(step - 2), held
        )
        if out is not None:
            recvs[step] = lax.ppermute(out, "section", [(0, 1), (1, 0)])
    late = [recvs[k + 2] for k in range(slots)]

    half = ff // 2
    down = [down_gradient(c, half, sc, late, cotangent, held["a"]) for c in (0, half)]
    up_jobs = [(0, 1, j * width) for j in range(blocks)]
    up = [
        products(up_jobs[: blocks // 2], sc, [held["n2"], held["gu"]], "w_up_grad_0"),
        products(up_jobs[blocks // 2 :], sc, [held["n2"], held["gu"]], "w_up_grad_1"),
    ]
    attn_sources = [held["o"], held["grb"], held["n1"], held["gqkv"]]
    attn = [
        products([(0, 1, 0), (2, 3, 0)], sc, attn_sources, "w_out_qkv_grad_0"),
        products(
            [(0, 1, width), (0, 1, 2 * width)], sc, [held["n1"], held["gqkv"]], "w_qkv_grad_1"
        ),
    ]
    summed = [sum_over_dp(*pair) for pair in down + up + attn]

    small = jnp.sum(held["small"], 0)
    grad_bup = jnp.sum(held["gu"].astype(F32), (0, 1))
    live = jnp.arange(seq)[None, :] < lengths[:, None]
    grad_bdown = jnp.sum(
        jnp.where(
            section == 0,
            jnp.stack(late).astype(F32),
            jnp.where(live[:, :, None], cotangent, jnp.zeros_like(cotangent)).astype(F32),
        ),
        (0, 1),
    )
    vector = jnp.concatenate([small[0], grad_bup, grad_bdown])
    n = lax.axis_size("dp")
    bit = 1
    while bit < n:
        vector = vector + lax.ppermute(vector, "dp", [(i, i ^ bit) for i in range(n)])
        bit *= 2

    quarter = width // 4
    parts = [p for pair in summed for p in pair]
    at = 1 + slots

    def plan_of(chunk, block, out, out_row, col):
        return [(2 * chunk + side, block * quarter, quarter, out, out_row, col) for side in (0, 1)]

    plan = []
    for b in range(blocks):
        plan += plan_of(b // (blocks // 2), b % (blocks // 2), 0, b * width, 0)
    (grad_wdown,) = unpack(plan, sc, at, parts[:4], [(ff, width)], "unpack_down")
    plan = []
    for b in range(blocks):
        plan += plan_of(b // (blocks // 2), b % (blocks // 2), 0, 0, b * width)
    (grad_wup,) = unpack(plan, sc, at, parts[4:8], [(width, ff)], "unpack_up")
    plan = (
        plan_of(0, 0, 0, 0, 0)
        + plan_of(0, 1, 1, 0, 0)
        + plan_of(1, 0, 1, 0, width)
        + plan_of(1, 1, 1, 0, 2 * width)
    )
    grad_wout, grad_wqkv = unpack(
        plan, sc, at, parts[8:12], [(width, width), (width, 3 * width)], "unpack_attn"
    )
    norm = vector[: 4 * width].reshape(2, 2, width)
    return (
        held["outputs"][None],
        held["grads"][None],
        norm[:, 0][None],
        norm[:, 1][None],
        grad_wqkv[None],
        grad_wout[None],
        grad_wup[None],
        vector[4 * width : 4 * width + ff][None],
        grad_wdown[None],
        vector[4 * width + ff :][None],
    )


def solution(mesh):
    placed = (
        P("dp", None, None),
        P("dp"),
        P("dp", None, None),
        P("section", None, None),
        P("section", None, None),
        P("section", None, None),
        P("section", None, None),
        P("section", None, None),
        P("section", None),
        P("section", None, None),
        P("section", None),
    )
    return jax.shard_map(
        per_device,
        mesh=mesh,
        in_specs=placed,
        out_specs=(
            P("section", "dp", None, None),
            P("section", "dp", None, None),
            P("section", None, None),
            P("section", None, None),
            P("section", None, None),
            P("section", None, None),
            P("section", None, None),
            P("section", None),
            P("section", None, None),
            P("section", None),
        ),
        check_vma=False,
    )
```

```python
import functools

import jax
import jax.numpy as jnp
from jax import lax
from jax.experimental import pallas as pl
from jax.experimental.pallas import tpu as pltpu
from jax.sharding import PartitionSpec as P

BF = jnp.bfloat16
F32 = jnp.float32
HEAD = 64
GROUP = 4
EPS = 1e-05
GELU_C = 0.7978845608028654
GELU_K = 0.044715
STEP_VMEM = 10 * 2**20


def dot(a, b):
    return lax.dot_general(a, b, (((1,), (0,)), ((), ())), preferred_element_type=F32)


def dot_t(a, b):
    return lax.dot_general(a, b, (((1,), (1,)), ((), ())), preferred_element_type=F32)


def t_dot(a, b):
    return lax.dot_general(a, b, (((0,), (0,)), ((), ())), preferred_element_type=F32)


def norm_parts(stream):
    mean = jnp.mean(stream, -1, keepdims=True)
    centred = stream - mean
    rstd = lax.rsqrt(jnp.mean(centred * centred, -1, keepdims=True) + EPS)
    return centred * rstd, rstd


def norm_back(hat, rstd, gain, grad):
    scaled = grad * gain
    a = jnp.mean(scaled, -1, keepdims=True)
    b = jnp.mean(scaled * hat, -1, keepdims=True)
    return rstd * (scaled - a - hat * b)


def gelu_and_slope(u):
    w = GELU_C + (GELU_C * GELU_K) * (u * u)
    half = 0.5 + 0.5 * jnp.tanh(u * w)
    a = u * half
    slope = half + (a - a * half) * (6.0 * w - 4.0 * GELU_C)
    return a.astype(BF), slope.astype(BF)


def head_masks(rows, axis):
    shape = (rows, GROUP * HEAD) if axis == 1 else (GROUP * HEAD, rows)
    lane = lax.broadcasted_iota(jnp.int32, shape, axis)
    return [(lane >= h * HEAD) & (lane < (h + 1) * HEAD) for h in range(GROUP)]


def layer_forward(x, limit, vec, s, wait):
    seq, width = x.shape
    ff = s["wup"].shape[1]
    gw = GROUP * HEAD
    hat, _ = norm_parts(x)
    n1 = (hat * vec[0:1, 0:width] + vec[0:1, width : 2 * width]).astype(BF)
    s["n1"][...] = n1
    wait("wqkv")
    s["qkv"][...] = dot(n1, s["wqkv"][...]).astype(BF)
    lane_masks = head_masks(seq, 1)
    row_masks = head_masks(seq, 0)
    key_bias = jnp.where(lax.broadcasted_iota(jnp.int32, (seq, 1), 0) < limit, 0.0, -1e30)
    for g in range(width // gw):
        q = s["qkv"][:, g * gw : (g + 1) * gw] * BF(HEAD**-0.5)
        k = s["qkv"][:, width + g * gw : width + (g + 1) * gw]
        v_t = s["qkv"][:, 2 * width + g * gw : 2 * width + (g + 1) * gw].T
        zero = jnp.zeros_like(q)
        mixed = jnp.zeros((gw, seq), F32)
        for h in range(GROUP):
            scores = dot_t(k, jnp.where(lane_masks[h], q, zero)) + key_bias
            e = jnp.exp(scores - jnp.max(scores, 0, keepdims=True))
            p = (e * (1.0 / jnp.sum(e, 0, keepdims=True))).astype(BF)
            s["pt"][g, :, h * seq : (h + 1) * seq] = p
            mixed = jnp.where(row_masks[h], dot(v_t, p), mixed)
        s["o"][:, g * gw : (g + 1) * gw] = mixed.T.astype(BF)
    wait("wout")
    r = x + dot(s["o"][...], s["wout"][...])
    s["r"][...] = r
    hat, _ = norm_parts(r)
    n2 = (hat * vec[0:1, 2 * width : 3 * width] + vec[0:1, 3 * width : 4 * width]).astype(BF)
    s["n2"][...] = n2
    wait("wup")
    for j in range(ff // width):
        cols = slice(j * width, (j + 1) * width)
        a, slope = gelu_and_slope(dot(n2, s["wup"][:, cols]) + vec[1:2, cols])
        s["a"][:, cols] = a
        s["d"][:, cols] = slope
    wait("wdn")
    y = s["r"][...] + vec[2:3, 0:width] + dot(s["a"][...], s["wdn"][...])
    return y.astype(BF)


def layer_backward(x, gy, vec, s, wait):
    seq, width = x.shape
    ff = s["wup"].shape[1]
    gw = GROUP * HEAD
    gyf = gy.astype(F32)
    wait("wdn")
    wait("d")
    for j in range(ff // width):
        cols = slice(j * width, (j + 1) * width)
        gu = dot_t(gy, s["wdn"][cols, :]) * s["d"][:, cols].astype(F32)
        s["gu"][:, cols] = gu.astype(BF)
    wait("wup")
    acc = dot_t(s["gu"][...], s["wup"][...])
    wait("r")
    hat, rstd = norm_parts(s["r"][...])
    s["small"][0:1, 2 * width : 3 * width] = jnp.sum(acc * hat, 0, keepdims=True)
    s["small"][0:1, 3 * width : 4 * width] = jnp.sum(acc, 0, keepdims=True)
    gr = gyf + norm_back(hat, rstd, vec[0:1, 2 * width : 3 * width], acc)
    grb = gr.astype(BF)
    s["grb"][...] = grb
    s["r"][...] = gr
    wait("wout")
    s["go"][...] = dot_t(grb, s["wout"][...]).astype(BF)
    lane_masks = head_masks(seq, 1)
    row_masks = head_masks(seq, 0)
    wait("qkv")
    wait("pt")
    for g in range(width // gw):
        q = s["qkv"][:, g * gw : (g + 1) * gw] * BF(HEAD**-0.5)
        k_t = s["qkv"][:, width + g * gw : width + (g + 1) * gw].T
        v = s["qkv"][:, 2 * width + g * gw : 2 * width + (g + 1) * gw]
        go = s["go"][:, g * gw : (g + 1) * gw]
        zero = jnp.zeros_like(q)
        gq = jnp.zeros((gw, seq), F32)
        for h in range(GROUP):
            cols = slice(h * seq, (h + 1) * seq)
            p = s["pt"][g, :, cols].astype(F32)
            go_h = jnp.where(lane_masks[h], go, zero)
            s["gos"][cols, :] = go_h
            s["qs"][cols, :] = jnp.where(lane_masks[h], q, zero)
            gp = dot_t(v, go_h)
            gs = (p * (gp - jnp.sum(gp * p, 0, keepdims=True))).astype(BF)
            s["gst"][:, cols] = gs
            gq = jnp.where(row_masks[h], dot(k_t, gs), gq)
        s["gqkv"][:, g * gw : (g + 1) * gw] = (gq.T * HEAD**-0.5).astype(BF)
        s["gqkv"][:, width + g * gw : width + (g + 1) * gw] = dot(
            s["gst"][...], s["qs"][...]
        ).astype(BF)
        s["gqkv"][:, 2 * width + g * gw : 2 * width + (g + 1) * gw] = dot(
            s["pt"][g], s["gos"][...]
        ).astype(BF)
    wait("wqkv")
    gn = dot_t(s["gqkv"][...], s["wqkv"][...])
    hat, rstd = norm_parts(x)
    s["small"][0:1, 0:width] = jnp.sum(gn * hat, 0, keepdims=True)
    s["small"][0:1, width : 2 * width] = jnp.sum(gn, 0, keepdims=True)
    return (s["r"][...] + norm_back(hat, rstd, vec[0:1, 0:width], gn)).astype(BF)


WEIGHTS = ("wqkv", "wout", "wup", "wdn")
LOADED = WEIGHTS + ("inputs", "cotangent")
STORES = (
    ("qkv", "pt", "r", "d")
    + ("n1", "n2", "o", "a")
    + ("gu", "grb", "gqkv", "small")
    + ("outputs", "grads")
)
VMEM = pl.BlockSpec(memory_space=pltpu.VMEM)
SMEM = pl.BlockSpec(memory_space=pltpu.SMEM)
HBM = pl.BlockSpec(memory_space=pltpu.HBM)


def in_vmem(value):
    return pltpu.with_memory_space_constraint(value, pltpu.VMEM)


def shapes_of(seq, width, ff):
    gw = GROUP * HEAD
    return {
        "qkv": ((seq, 3 * width), BF),
        "pt": ((width // gw, seq, GROUP * seq), BF),
        "r": ((seq, width), F32),
        "d": ((seq, ff), BF),
        "n1": ((seq, width), BF),
        "n2": ((seq, width), BF),
        "o": ((seq, width), BF),
        "a": ((seq, ff), BF),
        "gu": ((seq, ff), BF),
        "grb": ((seq, width), BF),
        "gqkv": ((seq, 3 * width), BF),
        "small": ((8, 4 * width), F32),
        "outputs": ((seq, width), BF),
        "grads": ((seq, width), BF),
    }


def step_body(step, slots, names, *refs):
    ref = dict(zip(names, refs))
    sc = ref["sc"]
    first = sc[0] == 0
    vec = ref["vec"]

    def view(slot):
        s = {k: ref["held_" + k].at[slot] for k in STORES}
        for k in WEIGHTS + ("go", "gst", "qs", "gos"):
            if k in ref:
                s[k] = ref[k]
        return s

    def ready(name):
        return None

    if step == 0:
        sems = ref["sems"]
        copies = {
            k: pltpu.make_async_copy(ref["hbm_" + k], ref[k], sems.at[i])
            for i, k in enumerate(LOADED)
        }
        get_x = pltpu.make_async_copy(ref["hbm_inputs"].at[0], ref["x"], sems.at[len(LOADED)])
        get_x.start()
        for k in LOADED:
            copies[k].start()
        get_x.wait()

        @pl.when(first)
        def _():
            s = view(0)
            y = layer_forward(
                ref["x"][...].astype(F32),
                jnp.maximum(sc[1], 1),
                vec,
                s,
                lambda name: copies[name].wait(),
            )
            s["outputs"][...] = y
            ref["send"][...] = y

        @pl.when(jnp.logical_not(first))
        def _():
            for k in WEIGHTS:
                copies[k].wait()

        copies["inputs"].wait()
        copies["cotangent"].wait()
        return

    if step < slots:

        @pl.when(first)
        def _():
            s = view(step)
            y = layer_forward(
                ref["inputs"][step].astype(F32), jnp.maximum(sc[1 + step], 1), vec, s, ready
            )
            s["outputs"][...] = y
            ref["send"][...] = y

    if "recv" in ref and step < slots + 2:

        @pl.when(jnp.logical_not(first))
        def _():
            slot = step - 2
            s = view(slot)
            length = sc[1 + slot]
            s["outputs"][...] = layer_forward(
                ref["recv"][...].astype(F32), jnp.maximum(length, 1), vec, s, ready
            )
            gy = ref["cotangent"][slot]
            live = lax.broadcasted_iota(jnp.int32, gy.shape, 0) < length
            gy = jnp.where(live, gy, jnp.zeros_like(gy))
            gx = layer_backward(ref["recv"][...].astype(F32), gy, vec, s, ready)
            s["grads"][...] = gx
            ref["send"][...] = gx

    if "recv" in ref and step >= slots:

        @pl.when(first)
        def _():
            slot = step - slots
            s = view(slot)
            s["grads"][...] = layer_backward(
                ref["inputs"][slot].astype(F32), ref["recv"][...], vec, s, ready
            )


def pipeline_step(step, sc, vec, weights, inputs, cotangent, recv, held, token):
    slots, seq, width = inputs.shape
    ff = weights["wup"].shape[1]
    shapes = shapes_of(seq, width, ff)
    names, args, specs = [], [], []
    out_names, out_shape, aliases = [], [], {}

    def give(name, value, spec):
        names.append(name)
        args.append(value)
        specs.append(spec)

    give("sc", sc, SMEM)
    give("vec", vec, VMEM)
    for name in STORES:
        shape, kind = shapes[name]
        out_names.append("held_" + name)
        out_shape.append(pltpu.VMEM((slots,) + shape, kind))
    if step == 0:
        sources = dict(weights, inputs=inputs, cotangent=cotangent)
        for name in LOADED:
            value = pltpu.with_memory_space_constraint(sources[name], pltpu.HBM)
            give("hbm_" + name, value, HBM)
            out_names.append(name)
            out_shape.append(pltpu.VMEM(value.shape, BF))
    else:
        for name in LOADED:
            give(name, in_vmem(held[name]), VMEM)
        give("token", in_vmem(token), VMEM)
        if recv is not None:
            give("recv", in_vmem(recv), VMEM)
        for i, name in enumerate(STORES):
            aliases[len(args)] = i
            give("in_" + name, in_vmem(held[name]), VMEM)
    out_names.append("token_out")
    out_shape.append(pltpu.VMEM((8, 128), F32))
    sends = step < slots + 2
    if sends:
        out_names.append("send")
        out_shape.append(pltpu.VMEM((seq, width), BF))
    gw = GROUP * HEAD
    scratch = {}
    if step == 0:
        scratch["x"] = pltpu.VMEM((seq, width), BF)
        scratch["sems"] = pltpu.SemaphoreType.DMA((len(LOADED) + 1,))
    if step >= 2:
        scratch["go"] = pltpu.VMEM((seq, width), BF)
        scratch["gst"] = pltpu.VMEM((seq, GROUP * seq), BF)
        scratch["qs"] = pltpu.VMEM((GROUP * seq, gw), BF)
        scratch["gos"] = pltpu.VMEM((GROUP * seq, gw), BF)
    out = pl.pallas_call(
        functools.partial(step_body, step, slots, names + out_names + list(scratch)),
        in_specs=specs,
        out_specs=[VMEM] * len(out_shape),
        out_shape=out_shape,
        scratch_shapes=list(scratch.values()),
        input_output_aliases=aliases,
        compiler_params=pltpu.CompilerParams(vmem_limit_bytes=STEP_VMEM),
        cost_estimate=pl.CostEstimate(
            flops=4 * seq * (width * 4 * width + 2 * width * ff),
            bytes_accessed=2**20,
            transcendentals=0,
        ),
        name=f"step_{step}",
    )(*args)
    result = dict(zip(out_names, out))
    new = {name: result["held_" + name] for name in STORES}
    for name in LOADED:
        new[name] = result[name] if step == 0 else held[name]
    return new, result.get("send"), result["token_out"]


def small_call(name, body, sc, ins, outs, token, flops=0, scratch=(), hbm_outs=0):
    n_in, n_out = len(ins), len(outs)

    def wrapped(sc_ref, token_ref, *refs):
        body(sc_ref, *refs[:n_in], *refs[n_in : n_in + n_out], *refs[n_in + n_out + 1 :])

    out = pl.pallas_call(
        wrapped,
        in_specs=[SMEM] + [VMEM] * (1 + n_in),
        out_specs=[VMEM] * (n_out - hbm_outs) + [HBM] * hbm_outs + [VMEM],
        out_shape=list(outs) + [pltpu.VMEM((8, 128), F32)],
        scratch_shapes=list(scratch),
        compiler_params=pltpu.CompilerParams(vmem_limit_bytes=STEP_VMEM),
        cost_estimate=pl.CostEstimate(
            flops=flops, bytes_accessed=2**20, transcendentals=0
        ),
        name=name,
    )(sc, in_vmem(token), *[in_vmem(v) for v in ins])
    return out[:-1], out[-1]


def place_block(keep, send, sc, at, block_row, value):
    rows = value.shape[0] // 4
    value = value.astype(BF)
    for core in range(2):
        for row in range(2):
            part = value[(2 * core + row) * rows : (2 * core + row + 1) * rows, :]
            place = lax.bitwise_xor(row, sc[at + 1])

            @pl.when(sc[at] == core)
            def _(part=part, place=place):
                keep[place, block_row : block_row + rows, :] = part

            @pl.when(sc[at] != core)
            def _(part=part, place=place):
                send[place, block_row : block_row + rows, :] = part


def chunk_shape(blocks, width, extra=0):
    return pltpu.VMEM((2, blocks * width // 4 + extra, width), BF)


def down_gradient(part, blocks, sc, recvs, cotangent, a, gm, token):
    slots, seq, width = cotangent.shape
    at = 1 + slots

    def products_of(sc_ref, a_ref, gm_ref, keep, send):
        for b in range(blocks):
            cols = slice((part * blocks + b) * width, (part * blocks + b + 1) * width)
            left = a_ref[:, :, cols].reshape(slots * seq, width)
            place_block(keep, send, sc_ref, at, b * (width // 4), t_dot(left, gm_ref[...]))

    def first(sc_ref, a_ref, cot, *rest):
        recv_refs = rest[:slots]
        keep, send, gm_ref, sums = rest[slots:]

        @pl.when(sc_ref[0] == 0)
        def _():
            for k in range(slots):
                gm_ref[k * seq : (k + 1) * seq, :] = recv_refs[k][...]

        @pl.when(sc_ref[0] != 0)
        def _():
            for k in range(slots):
                live = lax.broadcasted_iota(jnp.int32, (seq, width), 0) < sc_ref[1 + k]
                gm_ref[k * seq : (k + 1) * seq, :] = jnp.where(
                    live, cot[k], jnp.zeros((seq, width), BF)
                )

        products_of(sc_ref, a_ref, gm_ref, keep, send)
        sums[0:1, :] = jnp.sum(gm_ref[...].astype(F32), 0, keepdims=True)

    outs = [chunk_shape(blocks, width)] * 2
    flops = 2 * slots * seq * width * width * blocks
    name = f"w_down_grad_{part}"
    if gm is None:
        outs += [pltpu.VMEM((slots * seq, width), BF), pltpu.VMEM((8, width), F32)]
        return small_call(name, first, sc, [a, cotangent] + recvs, outs, token, flops)
    return small_call(name, products_of, sc, [a, gm], outs, token, flops)


def up_gradient(part, blocks, sc, n2, gu, token):
    slots, seq, width = n2.shape

    def body(sc_ref, n2_ref, gu_ref, keep, send, sums):
        left = n2_ref[...].reshape(slots * seq, width)
        for b in range(blocks):
            cols = slice((part * blocks + b) * width, (part * blocks + b + 1) * width)
            right = gu_ref[:, :, cols].reshape(slots * seq, width)
            place_block(keep, send, sc_ref, 1 + slots, b * (width // 4), t_dot(left, right))
            sums[0:1, b * width : (b + 1) * width] = jnp.sum(right.astype(F32), 0, keepdims=True)

    outs = [chunk_shape(blocks, width)] * 2 + [pltpu.VMEM((8, blocks * width), F32)]
    flops = 2 * slots * seq * width * width * blocks
    return small_call(f"w_up_grad_{part}", body, sc, [n2, gu], outs, token, flops)


def attention_gradient_0(sc, o, grb, n1, gqkv, token):
    slots, seq, width = o.shape

    def body(sc_ref, o_ref, grb_ref, n1_ref, gqkv_ref, keep, send):
        def rows(ref):
            return ref[...].reshape(slots * seq, width)

        place_block(keep, send, sc_ref, 1 + slots, 0, t_dot(rows(o_ref), rows(grb_ref)))
        right = gqkv_ref[:, :, 0:width].reshape(slots * seq, width)
        place_block(keep, send, sc_ref, 1 + slots, width // 4, t_dot(rows(n1_ref), right))

    outs = [chunk_shape(2, width)] * 2
    flops = 4 * slots * seq * width * width
    return small_call("w_out_q_grad", body, sc, [o, grb, n1, gqkv], outs, token, flops)


SMALL_ROWS = 16


def attention_gradient_1(sc, n1, gqkv, small, up_sums, down_sums, token):
    slots, seq, width = n1.shape

    def body(sc_ref, n1_ref, gqkv_ref, small_ref, up0, up1, down, keep, send, block):
        left = n1_ref[...].reshape(slots * seq, width)
        for b in (1, 2):
            right = gqkv_ref[:, :, b * width : (b + 1) * width].reshape(slots * seq, width)
            place_block(keep, send, sc_ref, 1 + slots, (b - 1) * (width // 4), t_dot(left, right))
        block[...] = jnp.zeros_like(block)
        norms = jnp.sum(small_ref[:, 0:1, :], 0)
        for i in range(4):
            block[i : i + 1, :] = norms[:, i * width : (i + 1) * width]
        row = 4
        for ref in (up0, up1):
            for i in range(ref.shape[1] // width):
                block[row : row + 1, :] = ref[0:1, i * width : (i + 1) * width]
                row += 1
        block[row : row + 1, :] = down[0:1, :]
        place_block(keep, send, sc_ref, 1 + slots, 2 * (width // 4), block[...])

    outs = [chunk_shape(2, width, SMALL_ROWS)] * 2
    return small_call(
        "w_kv_grad",
        body,
        sc,
        [n1, gqkv, small] + up_sums + [down_sums],
        outs,
        token,
        4 * slots * seq * width * width,
        [pltpu.VMEM((4 * SMALL_ROWS, width), F32)],
    )


def added(a, b):
    return (a[...].astype(F32) + b[...].astype(F32)).astype(BF)


def exchange(value, fn):
    n = lax.axis_size("dp")
    return lax.ppermute(value, "dp", [(i, fn(i)) for i in range(n)])


def other_core(i):
    return i ^ 1


def other_row(i):
    return i ^ 2


def z_pair(i):
    return i ^ 4


def z_middle(i):
    return {1: i + 4, 2: i - 4}.get(i // 4, i)


def after_cores(c, sc, keep, got, token):
    def body(sc_ref, keep_ref, got_ref, mine, other):
        mine[...] = added(keep_ref.at[0], got_ref.at[0])
        other[...] = added(keep_ref.at[1], got_ref.at[1])

    out = pltpu.VMEM(keep.shape[1:], BF)
    return small_call(f"after_cores_{c}", body, sc, [keep, got], [out, out], token)


def rows_of(*values):
    return max(v.shape[0] for v in values if v is not None)


def before_pair(i, sc, at, mine, got, part, got_middle, token):
    up, down = mine is not None, part is not None
    ins = ([mine, got] if up else []) + ([part, got_middle] if down else [])
    width = ins[0].shape[1]
    outs = [pltpu.VMEM(v.shape, BF) for v in ([mine] if up else []) + ([part] if down else [])]
    merged = up and down
    if merged:
        outs.append(pltpu.VMEM((rows_of(mine, part), width), BF))

    def body(sc_ref, *refs):
        refs = list(refs)
        sums = []
        for _ in range(int(up) + int(down)):
            sums.append(added(refs.pop(0), refs.pop(0)))
        for value in sums:
            refs.pop(0)[...] = value
        if merged:
            pay = refs.pop(0)
            for value, wanted in zip(sums, (1, 0)):

                @pl.when(sc_ref[at + 2] == wanted)
                def _(value=value):
                    pay[0 : value.shape[0], :] = value

    out, token = small_call(f"before_pair_{i}", body, sc, ins, outs, token)
    out = list(out)
    total_up = out.pop(0) if up else None
    total = out.pop(0) if down else None
    pay = out.pop(0) if merged else (total_up if up else total)
    return total_up, total, pay, token


def after_pair(i, sc, at, own, got, total, token):
    up, down = own is not None, total is not None
    ins = [got] + ([own] if up else []) + ([total] if down else [])
    outs = [pltpu.VMEM(v.shape, BF) for v in ([own] if up else []) + ([total] if down else [])]

    def body(sc_ref, got_ref, *refs):
        refs = list(refs)
        own_ref = refs.pop(0) if up else None
        total_ref = refs.pop(0) if down else None
        if up:
            out = refs.pop(0)
            out[...] = added(own_ref, got_ref.at[0 : out.shape[0]])
        if down:
            out = refs.pop(0)

            @pl.when(sc_ref[at + 2] == 1)
            def _():
                out[...] = got_ref[0 : out.shape[0], :]

            @pl.when(sc_ref[at + 2] == 0)
            def _():
                out[...] = total_ref[...]

    out, token = small_call(f"after_pair_{i}", body, sc, ins, outs, token)
    out = list(out)
    return (out.pop(0) if up else None), (out.pop(0) if down else None), token


def add_pair(name, sc, a, b, token):
    def body(sc_ref, a_ref, b_ref, out):
        out[...] = added(a_ref, b_ref)

    (out,), token = small_call(name, body, sc, [a, b], [pltpu.VMEM(a.shape, BF)], token)
    return out, token


def unpack(name, sc, at, plan, parts, out_shapes, token):
    n_parts = len(parts)
    width = parts[0].shape[1]
    staged = [(rows, width) for _, _, rows, _, _, _ in plan for _ in range(4)]

    def body(sc_ref, *refs):
        part_refs = refs[:n_parts]
        outs = refs[n_parts : n_parts + len(out_shapes)]
        stage, sems = refs[n_parts + len(out_shapes) :]
        position = 2 * sc_ref[at] + sc_ref[at + 1]
        copies = []
        done = 0
        for n, (chunk, row, rows, out, out_row, col) in enumerate(plan):
            for place in range(4):
                quarter = lax.bitwise_xor(position, place)
                target = pl.multiple_of(out_row + quarter * rows, rows)
                stage[done : done + rows, :] = part_refs[4 * chunk + place][
                    row : row + rows, :
                ].astype(F32)
                copy = pltpu.make_async_copy(
                    stage.at[done : done + rows],
                    outs[out].at[pl.ds(target, rows), col : col + width],
                    sems.at[4 * n + place],
                )
                copy.start()
                copies.append(copy)
                done += rows
        for copy in copies:
            copy.wait()

    total = sum(s[0] for s in staged)
    out, token = small_call(
        name,
        body,
        sc,
        parts,
        [jax.ShapeDtypeStruct(shape, F32) for shape in out_shapes],
        token,
        scratch=[pltpu.VMEM((total, width), F32), pltpu.SemaphoreType.DMA((len(staged),))],
        hbm_outs=len(out_shapes),
    )
    return out, token


def per_device(
    inputs,
    lengths,
    cotangent,
    norm_gain,
    layer_norm_biases,
    w_qkv,
    w_out,
    w_up,
    b_up,
    w_down,
    b_down,
):
    slots, seq, width = inputs.shape
    ff = w_up.shape[-1]
    blocks = ff // width
    half = blocks // 2
    at = 1 + slots
    section = lax.axis_index("section")
    place = lax.axis_index("dp")
    n_dp = lax.axis_size("dp")
    z = place // 4
    sc = jnp.concatenate(
        [
            jnp.stack([section]),
            lengths,
            jnp.stack([place % 2, (place // 2) % 2, ((z == 0) | (z == 3)).astype(jnp.int32)]),
        ]
    ).astype(jnp.int32)
    weights = {"wqkv": w_qkv[0], "wout": w_out[0], "wup": w_up[0], "wdn": w_down[0]}
    vec = jnp.zeros((8, ff), F32)
    norms = jnp.stack([norm_gain[0], layer_norm_biases[0]], 1).astype(F32).reshape(1, -1)
    vec = vec.at[0:1].set(norms)
    vec = vec.at[1:2].set(b_up.astype(F32))
    vec = vec.at[2:3, :width].set(b_down.astype(F32))

    held, recvs = None, {}

    def run_step(step, held, token):
        held, out, token = pipeline_step(
            step, sc, vec, weights, inputs, cotangent, recvs.get(step - 2), held, token
        )
        if out is not None:
            recvs[step] = lax.ppermute(out, "section", [(0, 1), (1, 0)])
        return held, token

    token = None
    for step in range(2 * slots - 1):
        held, token = run_step(step, held, token)
    late = [recvs[k + 2] for k in range(slots)]

    n_chunks = 6
    keep, mine, got_row = {}, {}, {}
    got_core, part, got_middle, own, total, full = {}, {}, {}, {}, {}, {}

    def begin(c, pair):
        keep[c], send = pair
        got_core[c] = exchange(send, other_core)

    def cores(c, token):
        (mine[c], other), token = after_cores(c, sc, keep[c], got_core[c], token)
        got_row[c] = exchange(other, other_row)
        return token

    def finish(c):
        other = exchange(full[c], other_row)
        full[c] = [full[c], other, exchange(full[c], other_core), exchange(other, other_core)]

    def up_down(i, token):
        up, down = i < n_chunks, i >= 2
        own[i], total[i - 2], pay, token = before_pair(
            i,
            sc,
            at,
            mine[i] if up else None,
            got_row[i] if up else None,
            part[i - 2] if down else None,
            got_middle[i - 2] if down else None,
            token,
        )
        return exchange(pay, z_pair), token

    def middle(i, got, token):
        part[i], full[i - 2], token = after_pair(
            i, sc, at, own[i], got, total.get(i - 2), token
        )
        if part[i] is not None:
            got_middle[i] = exchange(part[i], z_middle)
        if full[i - 2] is not None:
            finish(i - 2)
        return token

    (k0, s0, gm, down_sums), token = down_gradient(
        0, half, sc, late, held["cotangent"], held["a"], None, token
    )
    begin(0, (k0, s0))
    pair, token = down_gradient(
        1, half, sc, late, held["cotangent"], held["a"], gm, token
    )
    begin(1, pair)
    token = cores(0, token)
    held, token = run_step(2 * slots - 1, held, token)
    token = cores(1, token)
    (k2, s2, up_0), token = up_gradient(0, half, sc, held["n2"], held["gu"], token)
    begin(2, (k2, s2))
    pipelined = n_dp == 16
    got = {}
    if pipelined:
        got[0], token = up_down(0, token)
    (k3, s3, up_1), token = up_gradient(1, half, sc, held["n2"], held["gu"], token)
    begin(3, (k3, s3))
    token = cores(2, token)
    if pipelined:
        got[1], token = up_down(1, token)
        token = middle(0, got[0], token)
    pair, token = attention_gradient_0(
        sc, held["o"], held["grb"], held["n1"], held["gqkv"], token
    )
    begin(4, pair)
    token = cores(3, token)
    if pipelined:
        token = middle(1, got[1], token)
    pair, token = attention_gradient_1(
        sc, held["n1"], held["gqkv"], held["small"], [up_0, up_1], down_sums, token
    )
    begin(5, pair)
    token = cores(4, token)
    token = cores(5, token)
    if pipelined:
        for i in range(2, n_chunks + 2):
            got[i], token = up_down(i, token)
            token = middle(i, got[i], token)
    else:
        for c in range(n_chunks):
            value, token = add_pair(f"rows_{c}", sc, mine[c], got_row[c], token)
            bit = 4
            while bit < n_dp:
                other = exchange(value, lambda i, bit=bit: i ^ bit)
                value, token = add_pair(f"bit_{bit}_{c}", sc, value, other, token)
                bit *= 2
            full[c] = value
            finish(c)

    quarter = width // 4
    plan = [(b // half, (b % half) * quarter, quarter, 0, b * width, 0) for b in range(blocks)]
    (grad_wdown,), token = unpack(
        "unpack_down", sc, at, plan, full[0] + full[1], [(ff, width)], token
    )
    plan = [(b // half, (b % half) * quarter, quarter, 0, 0, b * width) for b in range(blocks)]
    (grad_wup,), token = unpack(
        "unpack_up", sc, at, plan, full[2] + full[3], [(width, ff)], token
    )
    plan = [
        (0, 0, quarter, 0, 0, 0),
        (0, quarter, quarter, 1, 0, 0),
        (1, 0, quarter, 1, 0, width),
        (1, quarter, quarter, 1, 0, 2 * width),
        (1, 2 * quarter, SMALL_ROWS, 2, 0, 0),
    ]
    (grad_wout, grad_wqkv, small), token = unpack(
        "unpack_attention",
        sc,
        at,
        plan,
        full[4] + full[5],
        [(width, width), (width, 3 * width), (4 * SMALL_ROWS, width)],
        token,
    )
    norm = small[0:4].reshape(2, 2, width)
    return (
        held["outputs"][None],
        held["grads"][None],
        norm[:, 0][None],
        norm[:, 1][None],
        grad_wqkv[None],
        grad_wout[None],
        grad_wup[None],
        small[4 : 4 + blocks].reshape(1, ff),
        grad_wdown[None],
        small[4 + blocks : 5 + blocks],
    )


def solution(mesh):
    placed = (
        P("dp", None, None),
        P("dp"),
        P("dp", None, None),
        P("section", None, None),
        P("section", None, None),
        P("section", None, None),
        P("section", None, None),
        P("section", None, None),
        P("section", None),
        P("section", None, None),
        P("section", None),
    )
    return jax.shard_map(
        per_device,
        mesh=mesh,
        in_specs=placed,
        out_specs=(
            P("section", "dp", None, None),
            P("section", "dp", None, None),
            P("section", None, None),
            P("section", None, None),
            P("section", None, None),
            P("section", None, None),
            P("section", None, None),
            P("section", None),
            P("section", None, None),
            P("section", None),
        ),
        check_vma=False,
    )
```

```python
import functools

import jax
import jax.numpy as jnp
from jax import lax
from jax.experimental import pallas as pl
from jax.experimental.pallas import tpu as pltpu
from jax.sharding import PartitionSpec as P

BF = jnp.bfloat16
F32 = jnp.float32
HEAD = 64
GROUP = 4
EPS = 1e-05
GELU_C = 0.7978845608028654
GELU_K = 0.044715
STEP_VMEM = 10 * 2**20
WIDTH = 512


def dot(a, b):
    return lax.dot_general(a, b, (((1,), (0,)), ((), ())), preferred_element_type=F32)


def dot_t(a, b):
    return lax.dot_general(a, b, (((1,), (1,)), ((), ())), preferred_element_type=F32)


def t_dot(a, b):
    return lax.dot_general(a, b, (((0,), (0,)), ((), ())), preferred_element_type=F32)


def norm_parts(stream):
    mean = jnp.mean(stream, -1, keepdims=True)
    centred = stream - mean
    rstd = lax.rsqrt(jnp.mean(centred * centred, -1, keepdims=True) + EPS)
    return centred * rstd, rstd


def norm_back(hat, rstd, gain, grad):
    scaled = grad * gain
    a = jnp.mean(scaled, -1, keepdims=True)
    b = jnp.mean(scaled * hat, -1, keepdims=True)
    return rstd * (scaled - a - hat * b)


def gelu_and_slope(u):
    w = GELU_C + (GELU_C * GELU_K) * (u * u)
    half = 0.5 + 0.5 * jnp.tanh(u * w)
    a = u * half
    slope = half + (a - a * half) * (6.0 * w - 4.0 * GELU_C)
    return a.astype(BF), slope.astype(BF)


def head_masks(rows, axis):
    shape = (rows, GROUP * HEAD) if axis == 1 else (GROUP * HEAD, rows)
    lane = lax.broadcasted_iota(jnp.int32, shape, axis)
    return [(lane >= h * HEAD) & (lane < (h + 1) * HEAD) for h in range(GROUP)]


def layer_forward(x, limit, vec, s, wait):
    seq, width = x.shape
    ff = s["wup"].shape[1]
    gw = GROUP * HEAD
    hat, _ = norm_parts(x)
    n1 = (hat * vec[0:1, 0:width] + vec[0:1, width : 2 * width]).astype(BF)
    s["n1"][...] = n1
    wait("wqkv")
    s["qkv"][...] = dot(n1, s["wqkv"][...]).astype(BF)
    lane_masks = head_masks(seq, 1)
    row_masks = head_masks(seq, 0)
    key_bias = jnp.where(lax.broadcasted_iota(jnp.int32, (seq, 1), 0) < limit, 0.0, -1e30)
    for g in range(width // gw):
        q = s["qkv"][:, g * gw : (g + 1) * gw] * BF(HEAD**-0.5)
        k = s["qkv"][:, width + g * gw : width + (g + 1) * gw]
        v_t = s["qkv"][:, 2 * width + g * gw : 2 * width + (g + 1) * gw].T
        zero = jnp.zeros_like(q)
        mixed = jnp.zeros((gw, seq), F32)
        for h in range(GROUP):
            scores = dot_t(k, jnp.where(lane_masks[h], q, zero)) + key_bias
            e = jnp.exp(scores - jnp.max(scores, 0, keepdims=True))
            p = (e * (1.0 / jnp.sum(e, 0, keepdims=True))).astype(BF)
            s["pt"][g, :, h * seq : (h + 1) * seq] = p
            mixed = jnp.where(row_masks[h], dot(v_t, p), mixed)
        s["o"][:, g * gw : (g + 1) * gw] = mixed.T.astype(BF)
    wait("wout")
    r = x + dot(s["o"][...], s["wout"][...])
    s["r"][...] = r
    hat, _ = norm_parts(r)
    n2 = (hat * vec[0:1, 2 * width : 3 * width] + vec[0:1, 3 * width : 4 * width]).astype(BF)
    s["n2"][...] = n2
    wait("wup")
    for j in range(ff // width):
        cols = slice(j * width, (j + 1) * width)
        a, slope = gelu_and_slope(dot(n2, s["wup"][:, cols]) + vec[1:2, cols])
        s["a"][:, cols] = a
        s["d"][:, cols] = slope
    wait("wdn")
    y = s["r"][...] + vec[2:3, 0:width] + dot(s["a"][...], s["wdn"][...])
    return y.astype(BF)


def layer_backward(x, gy, vec, s, started):
    seq, width = x.shape
    ff = s["wup"].shape[1]
    gw = GROUP * HEAD
    gyf = gy.astype(F32)
    if started:
        s["gu"][...] = s["gu"][...] * s["d"][...]
    else:
        for j in range(ff // width):
            cols = slice(j * width, (j + 1) * width)
            gu = dot_t(gy, s["wdn"][cols, :]) * s["d"][:, cols].astype(F32)
            s["gu"][:, cols] = gu.astype(BF)
    acc = dot_t(s["gu"][...], s["wup"][...])
    hat, rstd = norm_parts(s["r"][...])
    s["small"][0:1, 2 * width : 3 * width] = jnp.sum(acc * hat, 0, keepdims=True)
    s["small"][0:1, 3 * width : 4 * width] = jnp.sum(acc, 0, keepdims=True)
    gr = gyf + norm_back(hat, rstd, vec[0:1, 2 * width : 3 * width], acc)
    grb = gr.astype(BF)
    s["grb"][...] = grb
    s["r"][...] = gr
    s["go"][...] = dot_t(grb, s["wout"][...]).astype(BF)
    lane_masks = head_masks(seq, 1)
    row_masks = head_masks(seq, 0)
    for g in range(width // gw):
        q = s["qkv"][:, g * gw : (g + 1) * gw] * BF(HEAD**-0.5)
        k_t = s["qkv"][:, width + g * gw : width + (g + 1) * gw].T
        v = s["qkv"][:, 2 * width + g * gw : 2 * width + (g + 1) * gw]
        go = s["go"][:, g * gw : (g + 1) * gw]
        zero = jnp.zeros_like(q)
        gq = jnp.zeros((gw, seq), F32)
        for h in range(GROUP):
            cols = slice(h * seq, (h + 1) * seq)
            p = s["pt"][g, :, cols].astype(F32)
            go_h = jnp.where(lane_masks[h], go, zero)
            s["gos"][cols, :] = go_h
            s["qs"][cols, :] = jnp.where(lane_masks[h], q, zero)
            gp = dot_t(v, go_h)
            gs = (p * (gp - jnp.sum(gp * p, 0, keepdims=True))).astype(BF)
            s["gst"][:, cols] = gs
            gq = jnp.where(row_masks[h], dot(k_t, gs), gq)
        s["gqkv"][:, g * gw : (g + 1) * gw] = (gq.T * HEAD**-0.5).astype(BF)
        s["gqkv"][:, width + g * gw : width + (g + 1) * gw] = dot(
            s["gst"][...], s["qs"][...]
        ).astype(BF)
        s["gqkv"][:, 2 * width + g * gw : 2 * width + (g + 1) * gw] = dot(
            s["pt"][g], s["gos"][...]
        ).astype(BF)
    gn = dot_t(s["gqkv"][...], s["wqkv"][...])
    hat, rstd = norm_parts(x)
    s["small"][0:1, 0:width] = jnp.sum(gn * hat, 0, keepdims=True)
    s["small"][0:1, width : 2 * width] = jnp.sum(gn, 0, keepdims=True)
    return (s["r"][...] + norm_back(hat, rstd, vec[0:1, 0:width], gn)).astype(BF)


WEIGHTS = ("wqkv", "wout", "wup", "wdn")
LOADED = WEIGHTS + ("inputs", "cotangent")
VECTORS = ("gains", "biases", "b_up", "b_down")
STORES = (
    ("qkv", "pt", "r", "d")
    + ("n1", "n2", "o", "a")
    + ("gu", "grb", "gqkv", "small")
    + ("outputs", "grads")
)
VMEM = pl.BlockSpec(memory_space=pltpu.VMEM)
SMEM = pl.BlockSpec(memory_space=pltpu.SMEM)
HBM = pl.BlockSpec(memory_space=pltpu.HBM)


def in_vmem(value):
    return pltpu.with_memory_space_constraint(value, pltpu.VMEM)


def shapes_of(seq, width, ff):
    gw = GROUP * HEAD
    return {
        "qkv": ((seq, 3 * width), BF),
        "pt": ((width // gw, seq, GROUP * seq), BF),
        "r": ((seq, width), F32),
        "d": ((seq, ff), BF),
        "n1": ((seq, width), BF),
        "n2": ((seq, width), BF),
        "o": ((seq, width), BF),
        "a": ((seq, ff), BF),
        "gu": ((seq, ff), BF),
        "grb": ((seq, width), BF),
        "gqkv": ((seq, 3 * width), BF),
        "small": ((8, 4 * width), F32),
        "outputs": ((seq, width), BF),
        "grads": ((seq, width), BF),
    }


def step_body(step, slots, names, *refs):
    ref = dict(zip(names, refs))
    sc = ref["sc"]
    first = lax.axis_index("section") == 0
    second = jnp.logical_not(first)
    vec = ref["vec"]

    def view(slot):
        s = {k: ref["held_" + k].at[slot] for k in STORES}
        for k in WEIGHTS + ("go", "gst", "qs", "gos"):
            if k in ref:
                s[k] = ref[k]
        return s

    def ready(name):
        return None

    def row_gradient(slot):
        gy = ref["cotangent"][slot]
        live = lax.broadcasted_iota(jnp.int32, gy.shape, 0) < sc[slot]
        return jnp.where(live, gy, jnp.zeros_like(gy))

    def start_backward(slot):
        ref["held_gu"][slot] = dot_t(row_gradient(slot), ref["wdn"][...]).astype(BF)

    if step == 0:
        sems = ref["sems"]
        copies = {
            k: pltpu.make_async_copy(ref["hbm_" + k], ref[k], sems.at[i])
            for i, k in enumerate(LOADED)
        }
        more = [(ref["hbm_inputs"].at[0], ref["x"]), (ref["sc"], ref["lengths"])]
        more += [(ref["hbm_" + k], ref["v_" + k]) for k in VECTORS]
        more = [
            pltpu.make_async_copy(src, dst, sems.at[len(LOADED) + i])
            for i, (src, dst) in enumerate(more)
        ]
        for copy in more:
            copy.start()
        for k in LOADED:
            copies[k].start()
        for copy in more:
            copy.wait()
        width = ref["x"].shape[1]
        for i in range(2):
            for j, name in enumerate(("gains", "biases")):
                at = (2 * i + j) * width
                vec[0:1, at : at + width] = ref["v_" + name][i : i + 1, :].astype(F32)
        vec[1:2, :] = ref["v_b_up"][...].astype(F32)
        vec[2:3, 0:width] = ref["v_b_down"][...].astype(F32)
        sc = ref["lengths"]

        @pl.when(first)
        def _():
            s = view(0)
            y = layer_forward(
                ref["x"][...].astype(F32),
                jnp.maximum(sc[0], 1),
                vec,
                s,
                lambda name: copies[name].wait(),
            )
            s["outputs"][...] = y
            ref["send"][...] = y

        @pl.when(second)
        def _():
            for k in reversed(WEIGHTS):
                copies[k].wait()

        copies["inputs"].wait()
        copies["cotangent"].wait()

        @pl.when(second)
        def _():
            for slot in range(slots // 2):
                start_backward(slot)

        return

    if step >= slots and "recv" in ref:

        @pl.when(first)
        def _():
            slot = step - slots
            s = view(slot)
            s["grads"][...] = layer_backward(
                ref["inputs"][slot].astype(F32), ref["recv"][...], vec, s, False
            )

    if step == 1:

        @pl.when(second)
        def _():
            for slot in range(slots // 2, slots):
                start_backward(slot)

    if step < slots:

        @pl.when(first)
        def _():
            s = view(step)
            y = layer_forward(
                ref["inputs"][step].astype(F32), jnp.maximum(sc[step], 1), vec, s, ready
            )
            s["outputs"][...] = y
            ref["send"][...] = y

    if "recv" in ref and step < slots + 2:

        @pl.when(jnp.logical_not(first))
        def _():
            slot = step - 2
            s = view(slot)
            s["outputs"][...] = layer_forward(
                ref["recv"][...].astype(F32), jnp.maximum(sc[slot], 1), vec, s, ready
            )
            gx = layer_backward(ref["recv"][...].astype(F32), row_gradient(slot), vec, s, True)
            s["grads"][...] = gx
            ref["send"][...] = gx


def pipeline_step(step, sc, vectors, weights, inputs, cotangent, recv, held, token):
    slots, seq, width = inputs.shape
    ff = weights["wup"].shape[1]
    shapes = shapes_of(seq, width, ff)
    names, args, specs = [], [], []
    out_names, out_shape, aliases = [], [], {}

    def give(name, value, spec):
        names.append(name)
        args.append(value)
        specs.append(spec)

    give("sc", sc, HBM if step == 0 else SMEM)
    for name in STORES:
        shape, kind = shapes[name]
        out_names.append("held_" + name)
        out_shape.append(pltpu.VMEM((slots,) + shape, kind))
    if step == 0:
        for name, value in zip(VECTORS, vectors):
            give("hbm_" + name, pltpu.with_memory_space_constraint(value, pltpu.HBM), HBM)
        out_names.append("vec")
        out_shape.append(pltpu.VMEM((8, 4 * width), F32))
        sources = dict(weights, inputs=inputs, cotangent=cotangent)
        for name in LOADED:
            value = pltpu.with_memory_space_constraint(sources[name], pltpu.HBM)
            give("hbm_" + name, value, HBM)
            out_names.append(name)
            out_shape.append(pltpu.VMEM(value.shape, BF))
    else:
        for name in LOADED + ("vec",):
            give(name, in_vmem(held[name]), VMEM)
        give("token", in_vmem(token), VMEM)
        if recv is not None:
            give("recv", in_vmem(recv), VMEM)
        for i, name in enumerate(STORES):
            aliases[len(args)] = i
            give("in_" + name, in_vmem(held[name]), VMEM)
    out_names.append("token_out")
    out_shape.append(pltpu.VMEM((8, 128), F32))
    sends = step < slots + 2
    if sends:
        out_names.append("send")
        out_shape.append(pltpu.VMEM((seq, width), BF))
    gw = GROUP * HEAD
    scratch = {}
    if step == 0:
        scratch["x"] = pltpu.VMEM((seq, width), BF)
        scratch["lengths"] = pltpu.SMEM(sc.shape, jnp.int32)
        for name, value in zip(VECTORS, vectors):
            scratch["v_" + name] = pltpu.VMEM(value.shape, BF)
        scratch["sems"] = pltpu.SemaphoreType.DMA((len(LOADED) + 2 + len(VECTORS),))
    if step >= 2:
        scratch["go"] = pltpu.VMEM((seq, width), BF)
        scratch["gst"] = pltpu.VMEM((seq, GROUP * seq), BF)
        scratch["qs"] = pltpu.VMEM((GROUP * seq, gw), BF)
        scratch["gos"] = pltpu.VMEM((GROUP * seq, gw), BF)
    out = pl.pallas_call(
        functools.partial(step_body, step, slots, names + out_names + list(scratch)),
        in_specs=specs,
        out_specs=[VMEM] * len(out_shape),
        out_shape=out_shape,
        scratch_shapes=list(scratch.values()),
        input_output_aliases=aliases,
        compiler_params=pltpu.CompilerParams(vmem_limit_bytes=STEP_VMEM),
        cost_estimate=pl.CostEstimate(
            flops=4 * seq * (width * 4 * width + 2 * width * ff),
            bytes_accessed=2**20,
            transcendentals=0,
        ),
        name=f"step_{step}",
    )(*args)
    result = dict(zip(out_names, out))
    new = {name: result["held_" + name] for name in STORES}
    for name in LOADED + ("vec",):
        new[name] = result[name] if step == 0 else held[name]
    return new, result.get("send"), result["token_out"]


def small_call(name, body, sc, ins, outs, token, scratch=(), hbm_ins=(), hbm_outs=(), after=()):
    n_in, n_hbm, n_out = len(ins), len(hbm_ins), len(outs) + len(hbm_outs)
    skip = 1 + len(after)

    def wrapped(sc_ref, *refs):
        refs = refs[skip:]
        at = n_in + n_hbm
        body(sc_ref, *refs[:at], *refs[at : at + n_out], *refs[at + n_out + 1 :])

    first_hbm = 1 + skip + n_in
    out = pl.pallas_call(
        wrapped,
        in_specs=[SMEM] + [VMEM] * (skip + n_in) + [HBM] * n_hbm,
        out_specs=[VMEM] * len(outs) + [HBM] * len(hbm_outs) + [VMEM],
        out_shape=list(outs) + list(hbm_outs) + [pltpu.VMEM((8, 128), F32)],
        scratch_shapes=list(scratch),
        input_output_aliases={first_hbm + i: len(outs) + i for i in range(n_hbm)},
        compiler_params=pltpu.CompilerParams(vmem_limit_bytes=STEP_VMEM),
        cost_estimate=pl.CostEstimate(flops=0, bytes_accessed=0, transcendentals=0),
        name=name,
    )(
        sc,
        in_vmem(token),
        *[in_vmem(v) for v in after],
        *[in_vmem(v) for v in ins],
        *[pltpu.with_memory_space_constraint(v, pltpu.HBM) for v in hbm_ins],
    )
    return out[:-1], out[-1]


def place_block(keep, send, block_row, value):
    rows = value.shape[0] // 8
    value = value.astype(BF)
    place = lax.axis_index("dp")
    core, y, z = place % 2, (place // 2) % 2, (place // 4) % 2
    for eighth in range(8):
        c, row, parity = eighth // 4, (eighth // 2) % 2, eighth % 2
        part = value[eighth * rows : (eighth + 1) * rows, :]
        along_y, along_z = lax.bitwise_xor(row, y), lax.bitwise_xor(parity, z)
        at = 2 * along_y + along_z if c == 0 else 2 * along_z + along_y

        @pl.when(core == c)
        def _(part=part, at=at):
            keep[at, block_row : block_row + rows, :] = part

        @pl.when(core != c)
        def _(part=part, at=at):
            send[at, block_row : block_row + rows, :] = part


def chunk_shape(blocks, width, extra=0):
    return pltpu.VMEM((4, blocks * width // 8 + extra, width), BF)


def weight_gradients(name, sc, jobs, sources, token, recvs=None, sums_of=(), small=None, after=()):
    slots, seq, width = sources[-1].shape[0], sources[-1].shape[1], WIDTH
    n_src = len(sources)
    ins = list(sources) + list(recvs or []) + list(small or [])
    outs = [chunk_shape(len(jobs), width, SMALL_ROWS if small else 0)] * 2
    scratch = []
    if recvs:
        scratch.append(pltpu.VMEM((slots * seq, width), BF))
    if small:
        scratch.append(pltpu.VMEM((8 * SMALL_ROWS, width), F32))
    if sums_of:
        outs.append(pltpu.VMEM((8, len(sums_of) * width), F32))

    def body(sc_ref, *refs):
        refs = list(refs)
        src = [refs.pop(0) for _ in range(n_src)]
        recv_refs = [refs.pop(0) for _ in recvs or []]
        small_refs = [refs.pop(0) for _ in small or []]
        keep, send = refs.pop(0), refs.pop(0)
        sums = refs.pop(0) if sums_of else None
        gm = refs.pop(0) if recvs else None
        if recvs:
            first = lax.axis_index("section") == 0

            @pl.when(first)
            def _():
                for k in range(slots):
                    gm[k * seq : (k + 1) * seq, :] = recv_refs[k][...]

            @pl.when(jnp.logical_not(first))
            def _():
                for k in range(slots):
                    live = lax.broadcasted_iota(jnp.int32, (seq, width), 0) < sc_ref[k]
                    gm[k * seq : (k + 1) * seq, :] = jnp.where(
                        live, src[-1][k], jnp.zeros((seq, width), BF)
                    )

        def rows(ref, col):
            return ref[:, :, col : col + width].reshape(slots * seq, width)

        for n, (i, j, left_col, right_col) in enumerate(jobs):
            right = gm[...] if j is None else rows(src[j], right_col)
            block = t_dot(rows(src[i], left_col), right)
            place_block(keep, send, n * (width // 8), block)
            if n in sums_of:
                at = sums_of.index(n) * width
                sums[0:1, at : at + width] = jnp.sum(right.astype(F32), 0, keepdims=True)
        if small:
            block = refs.pop(0)
            block[...] = jnp.zeros_like(block)
            norms = jnp.sum(small_refs[0][:, 0:1, :], 0)
            row = 0
            for value in [norms] + [r[0:1, :] for r in small_refs[1:]]:
                for i in range(value.shape[1] // width):
                    block[row : row + 1, :] = value[:, i * width : (i + 1) * width]
                    row += 1
            place_block(keep, send, len(jobs) * (width // 8), block[...])

    return small_call(name, body, sc, ins, outs, token, scratch, after=after)


SMALL_ROWS = 16


def added(a, b):
    return (a[...].astype(F32) + b[...].astype(F32)).astype(BF)


def exchange(value, fn):
    n = lax.axis_size("dp")
    return lax.ppermute(value, "dp", [(i, fn(i)) for i in range(n)])


def other_core(i):
    return i ^ 1


def first_way(i):
    return i ^ 2 if i % 2 == 0 else i ^ 4


def second_way(i):
    return i ^ 4 if i % 2 == 0 else i ^ 2


def after_cores(c, sc, keep, got, token, after=()):
    def body(sc_ref, keep_ref, got_ref, mine, other):
        for p in range(2):
            mine[p] = added(keep_ref.at[p], got_ref.at[p])
            other[p] = added(keep_ref.at[2 + p], got_ref.at[2 + p])

    out = pltpu.VMEM((2,) + keep.shape[1:], BF)
    return small_call(f"after_cores_{c}", body, sc, [keep, got], [out, out], token, after=after)


def after_first(c, sc, mine, got, token, after=()):
    def body(sc_ref, mine_ref, got_ref, near, other):
        near[...] = added(mine_ref.at[0], got_ref.at[0])
        other[...] = added(mine_ref.at[1], got_ref.at[1])

    out = pltpu.VMEM(mine.shape[1:], BF)
    return small_call(f"after_first_{c}", body, sc, [mine, got], [out, out], token, after=after)


def add_pair(name, sc, a, b, token, after=()):
    def body(sc_ref, a_ref, b_ref, out):
        out[...] = added(a_ref, b_ref)

    out = [pltpu.VMEM(a.shape, BF)]
    (out,), token = small_call(name, body, sc, [a, b], out, token, after=after)
    return out, token


def stack_pair(name, sc, a, b, token, after=()):
    def body(sc_ref, a_ref, b_ref, out):
        out[0] = a_ref[...]
        out[1] = b_ref[...]

    out = [pltpu.VMEM((2,) + a.shape, BF)]
    (out,), token = small_call(name, body, sc, [a, b], out, token, after=after)
    return out, token


def unpack(name, sc, plan, parts, out_shapes, token, old=(), saved=(), small=None):
    n_parts, n_old, n_saved = len(parts), len(old), len(saved)
    width = parts[0].shape[-1]
    total = sum(8 * rows for _, rows, _, _, _ in plan)
    outs = list(old) + [jax.ShapeDtypeStruct(shape, F32) for shape in out_shapes]
    hbm_outs = [jax.ShapeDtypeStruct(v.shape, v.dtype) for v in outs + list(saved)]
    small_outs = []
    if small is not None:
        small_outs = [
            jax.ShapeDtypeStruct(shape, F32)
            for shape in ((1, 2, width), (1, 2, width), (1, small[1] * width), (1, width))
        ]
    n_copies = 8 * len(plan) + n_saved

    def body(sc_ref, *refs):
        refs = list(refs)
        part_refs = [refs.pop(0) for _ in range(n_parts)]
        saved_refs = [refs.pop(0) for _ in range(n_saved)]
        for _ in range(n_old):
            refs.pop(0)
        small_refs = [refs.pop(0) for _ in small_outs]
        out_refs = [refs.pop(0) for _ in outs]
        saved_out = [refs.pop(0) for _ in range(n_saved)]
        stage, sems = refs
        position = lax.axis_index("dp")
        core, y, z = position % 2, (position // 2) % 2, (position // 4) % 2
        copies = []

        def start(src, dst):
            copy = pltpu.make_async_copy(src, dst, sems.at[len(copies)])
            copy.start()
            copies.append(copy)

        for src, dst in zip(saved_refs, saved_out):
            start(src, dst)
        done = 0
        for row, rows, out, out_row, col in plan:
            for place in range(8):
                c = lax.bitwise_xor(core, place // 4)
                first, second = (place // 2) % 2, place % 2
                along_y = jnp.where(c == 0, first, second)
                along_z = jnp.where(c == 0, second, first)
                eighth = (
                    4 * c + 2 * lax.bitwise_xor(along_y, y) + lax.bitwise_xor(along_z, z)
                )
                part = part_refs[place // 2].at[place % 2]
                target = pl.multiple_of(out_row + eighth * rows, rows)
                stage[done : done + rows, :] = part[row : row + rows, :].astype(F32)
                start(
                    stage.at[done : done + rows],
                    out_refs[out].at[pl.ds(target, rows), col : col + width],
                )
                done += rows
                if small is not None and row == plan[-1][0]:

                    @pl.when(eighth == 0)
                    def _(part=part):
                        at, n_up = small
                        rows_ref = part[at : at + SMALL_ROWS, :].astype(F32)
                        gains, biases, b_up, b_down = small_refs
                        for i in range(2):
                            gains[0, i : i + 1, :] = rows_ref[2 * i : 2 * i + 1, :]
                            biases[0, i : i + 1, :] = rows_ref[2 * i + 1 : 2 * i + 2, :]
                        for i in range(n_up):
                            b_up[:, i * width : (i + 1) * width] = rows_ref[4 + i : 5 + i, :]
                        b_down[...] = rows_ref[4 + n_up : 5 + n_up, :]

        for copy in copies:
            copy.wait()

    return small_call(
        name,
        body,
        sc,
        list(parts) + list(saved),
        small_outs,
        token,
        scratch=[pltpu.VMEM((total, width), F32), pltpu.SemaphoreType.DMA((n_copies,))],
        hbm_ins=old,
        hbm_outs=hbm_outs,
    )


ORDER = "W0 S W1 A0 W2 A1 W3 B0 A2 B1 D0 D1 A3 B2 E0 B3 D2 E1 D3 F0 E2 F1 E3 F2 F3 U1 U0 U2 U3"
ARRIVED = {"F2": ("own", 3), "W3": ("first", 0)}


def per_device(
    inputs,
    lengths,
    cotangent,
    norm_gain,
    layer_norm_biases,
    w_qkv,
    w_out,
    w_up,
    b_up,
    w_down,
    b_down,
):
    slots, seq, width = inputs.shape
    ff = w_up.shape[-1]
    blocks = ff // width
    half = blocks // 2
    n_dp = lax.axis_size("dp")
    sc = lengths
    weights = {"wqkv": w_qkv[0], "wout": w_out[0], "wup": w_up[0], "wdn": w_down[0]}
    vectors = [norm_gain[0], layer_norm_biases[0], b_up, b_down]

    held, recvs = None, {}

    def run_step(step, held, token):
        held, out, token = pipeline_step(
            step, sc, vectors, weights, inputs, cotangent, recvs.get(step - 2), held, token
        )
        if out is not None:
            recvs[step] = lax.ppermute(out, "section", [(0, 1), (1, 0)])
        return held, token

    token = None
    for step in range(2 * slots - 1):
        held, token = run_step(step, held, token)
    late = [recvs[k + 2] for k in range(slots)]

    keep, got_core, mine, got_first, near, got_second = {}, {}, {}, {}, {}, {}
    total, got_far, own, got_own, got_back, got_parts = {}, {}, {}, {}, {}, {}
    eighth = width // 8
    down = [(0, None, b * width, 0) for b in range(blocks)]
    up = [(0, 1, 0, b * width) for b in range(blocks)]
    sums = {}
    arriving = {"first": got_first, "own": got_own}
    for op in ORDER.split():
        kind, c = op[0], int(op[1:] or 0)
        after = []
        if op in ARRIVED:
            after = [arriving[ARRIVED[op][0]][ARRIVED[op][1]]]
        if kind == "S":
            held, token = run_step(2 * slots - 1, held, token)
        elif kind == "W":
            if c == 0:
                sources = [held["a"], held["cotangent"]]
                out, token = weight_gradients(
                    "w_down_grad", sc, down, sources, token, recvs=late, sums_of=[0]
                )
            elif c == 1:
                sources = [held["n2"], held["gu"]]
                out, token = weight_gradients(
                    "w_up_grad", sc, up[:3], sources, token, sums_of=[0, 1, 2], after=after
                )
            elif c == 2:
                names = ("n2", "gu", "o", "grb", "gqkv", "n1")
                jobs = up[3:] + [(2, 3, 0, 0), (5, 4, 0, 0)]
                out, token = weight_gradients(
                    "w_up_out_q_grad",
                    sc,
                    jobs,
                    [held[k] for k in names],
                    token,
                    sums_of=[0],
                    after=after,
                )
            else:
                out, token = weight_gradients(
                    "w_kv_grad",
                    sc,
                    [(0, 1, 0, width), (0, 1, 0, 2 * width)],
                    [held["n1"], held["gqkv"]],
                    token,
                    small=[held["small"], sums[1], sums[2], sums[0]],
                    after=after,
                )
            keep[c], send = out[0], out[1]
            sums[c] = out[2] if len(out) > 2 else None
            got_core[c] = exchange(send, other_core)
        elif kind == "A":
            (mine[c], other), token = after_cores(c, sc, keep[c], got_core[c], token, after)
            got_first[c] = exchange(other, first_way)
        elif kind == "B":
            (near[c], other), token = after_first(c, sc, mine[c], got_first[c], token, after)
            got_second[c] = exchange(other, second_way)
        elif kind == "D":
            total[c], token = add_pair(
                f"after_second_{c}", sc, near[c], got_second[c], token, after
            )
            got_far[c] = exchange(total[c], lambda i: i ^ 8)
        elif kind == "E":
            value, token = add_pair(f"after_far_{c}", sc, total[c], got_far[c], token, after)
            bit = 16
            while bit < n_dp:
                other = exchange(value, lambda i, bit=bit: i ^ bit)
                value, token = add_pair(f"after_{bit}_{c}", sc, value, other, token)
                bit *= 2
            total[c] = value
            got_own[c] = exchange(value, second_way)
        elif kind == "F":
            own[c], token = stack_pair(f"pair_{c}", sc, total[c], got_own[c], token, after)
            got_back[c] = exchange(own[c], first_way)
            got_parts[c] = [exchange(own[c], other_core), exchange(got_back[c], other_core)]
        else:
            parts = [own[c], got_back[c]] + got_parts[c]
            if c == 0:
                plan = [(b * eighth, eighth, 0, b * width, 0) for b in range(blocks)]
                saved = [held["outputs"], held["grads"]]
                (grad_wdown, outputs, grads), token = unpack(
                    "unpack_down", sc, plan, parts, [(ff, width)], token, saved=saved
                )
            elif c == 1:
                plan = [(b * eighth, eighth, 0, 0, b * width) for b in range(3)]
                (grad_wup,), token = unpack("unpack_up", sc, plan, parts, [(width, ff)], token)
            elif c == 2:
                plan = [(b * eighth, eighth, 0, 0, (3 + b) * width) for b in range(blocks - 3)]
                at = (blocks - 3) * eighth
                plan += [(at, eighth, 1, 0, 0), (at + eighth, eighth, 2, 0, 0)]
                (grad_wup, grad_wout, grad_wqkv), token = unpack(
                    "unpack_up_out_q",
                    sc,
                    plan,
                    parts,
                    [(width, width), (width, 3 * width)],
                    token,
                    old=[grad_wup],
                )
            else:
                plan = [(b * eighth, eighth, 0, 0, (1 + b) * width) for b in range(2)]
                (gains, biases, grad_bup, grad_bdown, grad_wqkv), token = unpack(
                    "unpack_kv",
                    sc,
                    plan,
                    parts,
                    [],
                    token,
                    old=[grad_wqkv],
                    small=(2 * eighth, blocks),
                )
    return (
        outputs[None],
        grads[None],
        gains,
        biases,
        grad_wqkv[None],
        grad_wout[None],
        grad_wup[None],
        grad_bup,
        grad_wdown[None],
        grad_bdown,
    )


def solution(mesh):
    placed = (
        P("dp", None, None),
        P("dp"),
        P("dp", None, None),
        P("section", None, None),
        P("section", None, None),
        P("section", None, None),
        P("section", None, None),
        P("section", None, None),
        P("section", None),
        P("section", None, None),
        P("section", None),
    )
    return jax.shard_map(
        per_device,
        mesh=mesh,
        in_specs=placed,
        out_specs=(
            P("section", "dp", None, None),
            P("section", "dp", None, None),
            P("section", None, None),
            P("section", None, None),
            P("section", None, None),
            P("section", None, None),
            P("section", None, None),
            P("section", None),
            P("section", None, None),
            P("section", None),
        ),
        check_vma=False,
    )
```

```python
import functools

import jax
import jax.numpy as jnp
from jax import lax
from jax.experimental import pallas as pl
from jax.experimental.pallas import tpu as pltpu
from jax.sharding import PartitionSpec as P

SECTION, DP = "section", "dp"
BF = jnp.bfloat16
F32 = jnp.float32
HEAD = 64
GROUP = 4
EPS = 1e-05
GELU_C = 0.7978845608028654
GELU_K = 0.044715
STEP_VMEM = 10 * 2**20
WIDTH = 512


def dot(a, b):
    return lax.dot_general(a, b, (((1,), (0,)), ((), ())), preferred_element_type=F32)


def dot_t(a, b):
    return lax.dot_general(a, b, (((1,), (1,)), ((), ())), preferred_element_type=F32)


def t_dot(a, b):
    return lax.dot_general(a, b, (((0,), (0,)), ((), ())), preferred_element_type=F32)


def norm_parts(stream):
    mean = jnp.mean(stream, -1, keepdims=True)
    centred = stream - mean
    rstd = lax.rsqrt(jnp.mean(centred * centred, -1, keepdims=True) + EPS)
    return centred * rstd, rstd


def norm_back(hat, rstd, gain, grad):
    scaled = grad * gain
    a = jnp.mean(scaled, -1, keepdims=True)
    b = jnp.mean(scaled * hat, -1, keepdims=True)
    return rstd * (scaled - a - hat * b)


def gelu_and_slope(u):
    u = u.astype(BF)
    w = BF(GELU_C) + BF(GELU_C * GELU_K) * (u * u)
    t = BF(0.5) * jnp.tanh(u * w)
    half = BF(0.5) + t
    a = u * half
    return a, half + (a * (BF(0.5) - t)) * (BF(6.0) * w - BF(4.0 * GELU_C))


def head_masks(rows, axis):
    shape = (rows, GROUP * HEAD) if axis == 1 else (GROUP * HEAD, rows)
    lane = lax.broadcasted_iota(jnp.int32, shape, axis)
    return [(lane >= h * HEAD) & (lane < (h + 1) * HEAD) for h in range(GROUP)]


def head_parts(qkv, width):
    gw = GROUP * HEAD
    groups = range(width // gw)
    parts = [
        [qkv[:, j * width + g * gw : j * width + (g + 1) * gw] for g in groups] for j in range(3)
    ]
    parts[0] = [m * BF(HEAD**-0.5) for m in parts[0]]
    return [(g, h) for g in groups for h in range(GROUP)], parts


def layer_forward(x, limit, vec, s, wait):
    seq, width = x.shape
    ff = s["wup"].shape[1]
    gw = GROUP * HEAD
    hat, _ = norm_parts(x)
    n1 = (hat * vec[0:1, 0:width] + vec[0:1, width : 2 * width]).astype(BF)
    s["n1"][...] = n1
    wait("wqkv")
    s["qkv"][...] = dot(n1, s["wqkv"][...]).astype(BF)
    lane_masks = head_masks(seq, 1)
    key_bias = jnp.where(lax.broadcasted_iota(jnp.int32, (1, seq), 1) < limit, 0.0, -1e30)
    heads, (q, k, v) = head_parts(s["qkv"], width)
    zero = jnp.zeros_like(q[0])
    mixed = [jnp.zeros((seq, gw), F32) for _ in q]

    def scores_of(g, h):
        return dot_t(jnp.where(lane_masks[h], q[g], zero), k[g]) + key_bias

    def softmax_of(g, h, scores):
        e = jnp.exp(scores - jnp.max(scores, 1, keepdims=True))
        p = (e * (1.0 / jnp.sum(e, 1, keepdims=True))).astype(BF)
        s["pt"][g, :, h * seq : (h + 1) * seq] = p
        return p

    def mix(g, h, p):
        mixed[g] = jnp.where(lane_masks[h], dot(p, v[g]), mixed[g])

    scores, p = scores_of(*heads[0]), None
    for i, head in enumerate(heads):
        later = scores_of(*heads[i + 1]) if i + 1 < len(heads) else None
        last, p = p, softmax_of(*head, scores)
        if i > 0:
            mix(*heads[i - 1], last)
        scores = later
    mix(*heads[-1], p)
    for g in range(len(q)):
        s["o"][:, g * gw : (g + 1) * gw] = mixed[g].astype(BF)
    wait("wout")
    r = x + dot(s["o"][...], s["wout"][...])
    s["r"][...] = r
    hat, _ = norm_parts(r)
    n2 = (hat * vec[0:1, 2 * width : 3 * width] + vec[0:1, 3 * width : 4 * width]).astype(BF)
    s["n2"][...] = n2
    wait("wup")
    for j in range(ff // width):
        cols = slice(j * width, (j + 1) * width)
        a, slope = gelu_and_slope(dot(n2, s["wup"][:, cols]) + vec[1:2, cols])
        s["a"][:, cols] = a
        s["d"][:, cols] = slope
    wait("wdn")
    y = s["r"][...] + vec[2:3, 0:width] + dot(s["a"][...], s["wdn"][...])
    return y.astype(BF)


def layer_backward(x, gy, vec, s, started):
    seq, width = x.shape
    ff = s["wup"].shape[1]
    gw = GROUP * HEAD
    gyf = gy.astype(F32)
    if started:
        s["gu"][...] = s["gu"][...] * s["d"][...]
    else:
        for j in range(ff // width):
            cols = slice(j * width, (j + 1) * width)
            gu = dot_t(gy, s["wdn"][cols, :]) * s["d"][:, cols].astype(F32)
            s["gu"][:, cols] = gu.astype(BF)
    acc = dot_t(s["gu"][...], s["wup"][...])
    hat, rstd = norm_parts(s["r"][...])
    s["small"][0:1, 2 * width : 3 * width] = jnp.sum(acc * hat, 0, keepdims=True)
    s["small"][0:1, 3 * width : 4 * width] = jnp.sum(acc, 0, keepdims=True)
    gr = gyf + norm_back(hat, rstd, vec[0:1, 2 * width : 3 * width], acc)
    grb = gr.astype(BF)
    s["grb"][...] = grb
    s["r"][...] = gr
    s["go"][...] = dot_t(grb, s["wout"][...]).astype(BF)
    lane_masks = head_masks(seq, 1)
    row_masks = head_masks(seq, 0)
    heads, (q, k, v) = head_parts(s["qkv"], width)
    groups = range(len(q))
    go = [s["go"][:, g * gw : (g + 1) * gw] for g in groups]
    q_t, go_t = [m.T for m in q], [m.T for m in go]
    zero = jnp.zeros_like(q[0])
    gq = [jnp.zeros((seq, gw), F32) for _ in groups]
    gk_t = [jnp.zeros((gw, seq), F32) for _ in groups]
    gv_t = [jnp.zeros((gw, seq), F32) for _ in groups]

    def probs(g, h):
        return s["pt"][g, :, h * seq : (h + 1) * seq]

    def prob_gradient(g, h):
        return dot_t(jnp.where(lane_masks[h], go[g], zero), v[g])

    def score_gradient(g, h, gp):
        p = probs(g, h).astype(F32)
        return (p * (gp - jnp.sum(gp * p, 1, keepdims=True))).astype(BF)

    def spread(g, h, gs):
        gq[g] = jnp.where(lane_masks[h], dot(gs, k[g]), gq[g])
        gk_t[g] = jnp.where(row_masks[h], dot(q_t[g], gs), gk_t[g])

    gp, gs = prob_gradient(*heads[0]), None
    for i, (g, h) in enumerate(heads):
        later = prob_gradient(*heads[i + 1]) if i + 1 < len(heads) else None
        gv_t[g] = jnp.where(row_masks[h], dot(go_t[g], probs(g, h)), gv_t[g])
        last, gs = gs, score_gradient(g, h, gp)
        if i > 0:
            spread(*heads[i - 1], last)
        gp = later
    spread(*heads[-1], gs)
    for g in groups:
        cols = slice(g * gw, (g + 1) * gw)
        for part, value in enumerate((gq[g] * HEAD**-0.5, gk_t[g].T, gv_t[g].T)):
            s["gqkv"][:, part * width + g * gw : part * width + (g + 1) * gw] = value.astype(BF)
    gn = dot_t(s["gqkv"][...], s["wqkv"][...])
    hat, rstd = norm_parts(x)
    s["small"][0:1, 0:width] = jnp.sum(gn * hat, 0, keepdims=True)
    s["small"][0:1, width : 2 * width] = jnp.sum(gn, 0, keepdims=True)
    return (s["r"][...] + norm_back(hat, rstd, vec[0:1, 0:width], gn)).astype(BF)


WEIGHTS = ("wqkv", "wout", "wup", "wdn")
LOADED = WEIGHTS + ("inputs", "cotangent")
VECTORS = ("gains", "biases", "b_up", "b_down")
STORES = (
    ("qkv", "pt", "r", "d")
    + ("n1", "n2", "o", "a")
    + ("gu", "grb", "gqkv", "small")
    + ("outputs", "grads")
)
VMEM = pl.BlockSpec(memory_space=pltpu.VMEM)
SMEM = pl.BlockSpec(memory_space=pltpu.SMEM)
HBM = pl.BlockSpec(memory_space=pltpu.HBM)


def in_vmem(value):
    return pltpu.with_memory_space_constraint(value, pltpu.VMEM)


def shapes_of(seq, width, ff):
    gw = GROUP * HEAD
    return {
        "qkv": ((seq, 3 * width), BF),
        "pt": ((width // gw, seq, GROUP * seq), BF),
        "r": ((seq, width), F32),
        "d": ((seq, ff), BF),
        "n1": ((seq, width), BF),
        "n2": ((seq, width), BF),
        "o": ((seq, width), BF),
        "a": ((seq, ff), BF),
        "gu": ((seq, ff), BF),
        "grb": ((seq, width), BF),
        "gqkv": ((seq, 3 * width), BF),
        "small": ((8, 4 * width), F32),
        "outputs": ((seq, width), BF),
        "grads": ((seq, width), BF),
    }


def step_body(step, slots, names, *refs):
    ref = dict(zip(names, refs))
    sc = ref["sc"]
    first = lax.axis_index(SECTION) == 0
    second = jnp.logical_not(first)
    vec = ref["vec"]

    def view(slot):
        s = {k: ref["held_" + k].at[slot] for k in STORES}
        for k in WEIGHTS + ("go",):
            if k in ref:
                s[k] = ref[k]
        return s

    def ready(name):
        return None

    def row_gradient(slot):
        gy = ref["cotangent"][slot]
        live = lax.broadcasted_iota(jnp.int32, gy.shape, 0) < sc[slot]
        return jnp.where(live, gy, jnp.zeros_like(gy))

    def start_backward(slot):
        ref["held_gu"][slot] = dot_t(row_gradient(slot), ref["wdn"][...]).astype(BF)

    if step == 0:
        sems = ref["sems"]
        copies = {
            k: pltpu.make_async_copy(ref["hbm_" + k], ref[k], sems.at[i])
            for i, k in enumerate(LOADED)
        }
        more = [(ref["hbm_inputs"].at[0], ref["x"]), (ref["sc"], ref["lengths"])]
        more += [(ref["hbm_" + k], ref["v_" + k]) for k in VECTORS]
        more = [
            pltpu.make_async_copy(src, dst, sems.at[len(LOADED) + i])
            for i, (src, dst) in enumerate(more)
        ]
        for copy in more:
            copy.start()
        for k in LOADED:
            copies[k].start()
        for copy in more:
            copy.wait()
        width = ref["x"].shape[1]
        for i in range(2):
            for j, name in enumerate(("gains", "biases")):
                at = (2 * i + j) * width
                vec[0:1, at : at + width] = ref["v_" + name][i : i + 1, :].astype(F32)
        vec[1:2, :] = ref["v_b_up"][...].astype(F32)
        vec[2:3, 0:width] = ref["v_b_down"][...].astype(F32)
        sc = ref["lengths"]

        @pl.when(first)
        def _():
            s = view(0)
            y = layer_forward(
                ref["x"][...].astype(F32),
                jnp.maximum(sc[0], 1),
                vec,
                s,
                lambda name: copies[name].wait(),
            )
            s["outputs"][...] = y
            ref["send"][...] = y

        @pl.when(second)
        def _():
            for k in reversed(WEIGHTS):
                copies[k].wait()

        copies["inputs"].wait()
        copies["cotangent"].wait()

        @pl.when(second)
        def _():
            for slot in range(slots // 2):
                start_backward(slot)

        return

    if step >= slots and "recv" in ref:

        @pl.when(first)
        def _():
            slot = step - slots
            s = view(slot)
            s["grads"][...] = layer_backward(
                ref["inputs"][slot].astype(F32), ref["recv"][...], vec, s, False
            )

    if step == 1:

        @pl.when(second)
        def _():
            for slot in range(slots // 2, slots):
                start_backward(slot)

    if step < slots:

        @pl.when(first)
        def _():
            s = view(step)
            y = layer_forward(
                ref["inputs"][step].astype(F32), jnp.maximum(sc[step], 1), vec, s, ready
            )
            s["outputs"][...] = y
            ref["send"][...] = y

    if "recv" in ref and step < slots + 2:

        @pl.when(jnp.logical_not(first))
        def _():
            slot = step - 2
            s = view(slot)
            s["outputs"][...] = layer_forward(
                ref["recv"][...].astype(F32), jnp.maximum(sc[slot], 1), vec, s, ready
            )
            gx = layer_backward(ref["recv"][...].astype(F32), row_gradient(slot), vec, s, True)
            s["grads"][...] = gx
            ref["send"][...] = gx


def pipeline_step(step, sc, vectors, weights, inputs, cotangent, recv, held, token):
    slots, seq, width = inputs.shape
    ff = weights["wup"].shape[1]
    shapes = shapes_of(seq, width, ff)
    names, args, specs = [], [], []
    out_names, out_shape, aliases = [], [], {}

    def give(name, value, spec):
        names.append(name)
        args.append(value)
        specs.append(spec)

    give("sc", sc, HBM if step == 0 else SMEM)
    for name in STORES:
        shape, kind = shapes[name]
        out_names.append("held_" + name)
        out_shape.append(pltpu.VMEM((slots,) + shape, kind))
    if step == 0:
        for name, value in zip(VECTORS, vectors):
            give("hbm_" + name, pltpu.with_memory_space_constraint(value, pltpu.HBM), HBM)
        out_names.append("vec")
        out_shape.append(pltpu.VMEM((8, 4 * width), F32))
        sources = dict(weights, inputs=inputs, cotangent=cotangent)
        for name in LOADED:
            value = pltpu.with_memory_space_constraint(sources[name], pltpu.HBM)
            give("hbm_" + name, value, HBM)
            out_names.append(name)
            out_shape.append(pltpu.VMEM(value.shape, BF))
    else:
        for name in LOADED + ("vec",):
            give(name, in_vmem(held[name]), VMEM)
        give("token", in_vmem(token), VMEM)
        if recv is not None:
            give("recv", in_vmem(recv), VMEM)
        for i, name in enumerate(STORES):
            aliases[len(args)] = i
            give("in_" + name, in_vmem(held[name]), VMEM)
    out_names.append("token_out")
    out_shape.append(pltpu.VMEM((8, 128), F32))
    sends = step < slots + 2
    if sends:
        out_names.append("send")
        out_shape.append(pltpu.VMEM((seq, width), BF))
    scratch = {}
    if step == 0:
        scratch["x"] = pltpu.VMEM((seq, width), BF)
        scratch["lengths"] = pltpu.SMEM(sc.shape, jnp.int32)
        for name, value in zip(VECTORS, vectors):
            scratch["v_" + name] = pltpu.VMEM(value.shape, BF)
        scratch["sems"] = pltpu.SemaphoreType.DMA((len(LOADED) + 2 + len(VECTORS),))
    if step >= 2:
        scratch["go"] = pltpu.VMEM((seq, width), BF)
    out = pl.pallas_call(
        functools.partial(step_body, step, slots, names + out_names + list(scratch)),
        in_specs=specs,
        out_specs=[VMEM] * len(out_shape),
        out_shape=out_shape,
        scratch_shapes=list(scratch.values()),
        input_output_aliases=aliases,
        compiler_params=pltpu.CompilerParams(vmem_limit_bytes=STEP_VMEM),
        cost_estimate=pl.CostEstimate(
            flops=4 * seq * (width * 4 * width + 2 * width * ff),
            bytes_accessed=2**20,
            transcendentals=0,
        ),
        name=f"step_{step}",
    )(*args)
    result = dict(zip(out_names, out))
    new = {name: result["held_" + name] for name in STORES}
    for name in LOADED + ("vec",):
        new[name] = result[name] if step == 0 else held[name]
    return new, result.get("send"), result["token_out"]


def small_call(
    name, body, sc, ins, outs, token, scratch=(), hbm_ins=(), hbm_outs=(), after=(), flops=0
):
    n_in, n_hbm, n_out = len(ins), len(hbm_ins), len(outs) + len(hbm_outs)
    skip = 1 + len(after)

    def wrapped(sc_ref, *refs):
        refs = refs[skip:]
        at = n_in + n_hbm
        body(sc_ref, *refs[:at], *refs[at : at + n_out], *refs[at + n_out + 1 :])

    first_hbm = 1 + skip + n_in
    out = pl.pallas_call(
        wrapped,
        in_specs=[SMEM] + [VMEM] * (skip + n_in) + [HBM] * n_hbm,
        out_specs=[VMEM] * len(outs) + [HBM] * len(hbm_outs) + [VMEM],
        out_shape=list(outs) + list(hbm_outs) + [pltpu.VMEM((8, 128), F32)],
        scratch_shapes=list(scratch),
        input_output_aliases={first_hbm + i: len(outs) + i for i in range(n_hbm)},
        compiler_params=pltpu.CompilerParams(vmem_limit_bytes=STEP_VMEM),
        cost_estimate=pl.CostEstimate(flops=flops, bytes_accessed=0, transcendentals=0),
        name=name,
    )(
        sc,
        in_vmem(token),
        *[in_vmem(v) for v in after],
        *[in_vmem(v) for v in ins],
        *[pltpu.with_memory_space_constraint(v, pltpu.HBM) for v in hbm_ins],
    )
    return out[:-1], out[-1]


def place_eighths(places, block_row, block):
    keep, near, away = places
    rows = block.shape[0] // 8
    place = lax.axis_index(DP)
    core, y, z = place % 2, (place // 2) % 2, (place // 4) % 2
    for mine, c in ((True, core), (False, 1 - core)):
        for at in range(4):
            first, second = at // 2, at % 2
            target, to = (keep, at) if mine else (away if first else near, second)
            along_y = jnp.where(c == 0, first, second)
            along_z = jnp.where(c == 0, second, first)
            eighth = 4 * c + 2 * lax.bitwise_xor(along_y, y) + lax.bitwise_xor(along_z, z)
            source = pl.multiple_of(eighth * rows, rows)
            target[to, block_row : block_row + rows, :] = block[pl.ds(source, rows), :]


def chunk_shapes(blocks, width, extra=0):
    rows = blocks * width // 8 + extra
    return [pltpu.VMEM((n, rows, width), BF) for n in (4, 2, 2)]


def weight_gradients(
    name, sc, jobs, sources, token, recvs=None, sums_of=(), small=None, saved=(), after=()
):
    slots, seq, width = sources[-1].shape[0], sources[-1].shape[1], WIDTH
    n_src = len(sources)
    ins = list(sources) + list(recvs or []) + list(small or []) + list(saved)
    outs = chunk_shapes(len(jobs), width, SMALL_ROWS if small else 0)
    scratch = [pltpu.VMEM((len(jobs), width, width), BF)]
    if recvs:
        scratch.append(pltpu.VMEM((slots * seq, width), BF))
    if small:
        scratch.append(pltpu.VMEM((8 * SMALL_ROWS, width), F32))
        scratch.append(pltpu.VMEM((8 * SMALL_ROWS, width), BF))
    if sums_of:
        outs.append(pltpu.VMEM((8, len(sums_of) * width), F32))

    def body(sc_ref, *refs):
        refs = list(refs)
        src = [refs.pop(0) for _ in range(n_src)]
        recv_refs = [refs.pop(0) for _ in recvs or []]
        small_refs = [refs.pop(0) for _ in small or []]
        saved_refs = [refs.pop(0) for _ in saved]
        places = [refs.pop(0) for _ in range(3)]
        sums = refs.pop(0) if sums_of else None
        saved_outs = [refs.pop(0) for _ in saved]
        if saved:
            sems = refs.pop()
            copies = [
                pltpu.make_async_copy(src, dst, sems.at[i])
                for i, (src, dst) in enumerate(zip(saved_refs, saved_outs))
            ]
            for copy in copies:
                copy.start()
        blocks = refs.pop(0)
        gm = refs.pop(0) if recvs else None
        if recvs:
            first = lax.axis_index(SECTION) == 0

            @pl.when(first)
            def _():
                for k in range(slots):
                    gm[k * seq : (k + 1) * seq, :] = recv_refs[k][...]

            @pl.when(jnp.logical_not(first))
            def _():
                for k in range(slots):
                    live = lax.broadcasted_iota(jnp.int32, (seq, width), 0) < sc_ref[k]
                    gm[k * seq : (k + 1) * seq, :] = jnp.where(
                        live, src[-1][k], jnp.zeros((seq, width), BF)
                    )

        def rows(ref, col):
            return ref[:, :, col : col + width].reshape(slots * seq, width)

        for n, (i, j, left_col, right_col) in enumerate(jobs):
            right = gm[...] if j is None else rows(src[j], right_col)
            blocks[n] = t_dot(rows(src[i], left_col), right).astype(BF)
            if n in sums_of:
                at = sums_of.index(n) * width
                sums[0:1, at : at + width] = jnp.sum(right.astype(F32), 0, keepdims=True)
            if n > 0:
                place_eighths(places, (n - 1) * (width // 8), blocks.at[n - 1])
        place_eighths(places, (len(jobs) - 1) * (width // 8), blocks.at[len(jobs) - 1])
        if small:
            block = refs.pop(0)
            block[...] = jnp.zeros_like(block)
            norms = jnp.sum(small_refs[0][:, 0:1, :], 0)
            row = 0
            for value in [norms] + [r[0:1, :] for r in small_refs[1:]]:
                for i in range(value.shape[1] // width):
                    block[row : row + 1, :] = value[:, i * width : (i + 1) * width]
                    row += 1
            rounded = refs.pop(0)
            rounded[...] = block[...].astype(BF)
            place_eighths(places, len(jobs) * (width // 8), rounded)
        if saved:
            for copy in copies:
                copy.wait()

    if saved:
        scratch.append(pltpu.SemaphoreType.DMA((len(saved),)))
    hbm_outs = [jax.ShapeDtypeStruct(v.shape, v.dtype) for v in saved]
    return small_call(name, body, sc, ins, outs, token, scratch, hbm_outs=hbm_outs, after=after)


SMALL_ROWS = 16


def added(a, b):
    return (a[...].astype(F32) + b[...].astype(F32)).astype(BF)


def exchange(value, fn):
    n = lax.axis_size(DP)
    return lax.ppermute(value, DP, [(i, fn(i)) for i in range(n)])


def other_core(i):
    return i ^ 1


def first_way(i):
    return i ^ 2 if i % 2 == 0 else i ^ 4


def second_way(i):
    return i ^ 4 if i % 2 == 0 else i ^ 2


def added3(a, b, c):
    return (a[...].astype(F32) + b[...].astype(F32) + c[...].astype(F32)).astype(BF)


def after_cores(c, sc, keep, got, token, after=()):
    def body(sc_ref, keep_ref, got_ref, other):
        for p in range(2):
            other[p] = added(keep_ref.at[2 + p], got_ref.at[p])

    out = [pltpu.VMEM((2,) + keep.shape[1:], BF)]
    (out,), token = small_call(f"cores_{c}", body, sc, [keep, got], out, token, after=after)
    return out, token


def after_first(c, sc, keep, got_near, got, token, after=()):
    def body(sc_ref, keep_ref, core_ref, got_ref, near, other):
        near[...] = added3(keep_ref.at[0], core_ref.at[0], got_ref.at[0])
        other[...] = added3(keep_ref.at[1], core_ref.at[1], got_ref.at[1])

    out = pltpu.VMEM(keep.shape[1:], BF)
    ins = [keep, got_near, got]
    return small_call(f"first_{c}", body, sc, ins, [out, out], token, after=after)


def add_pair(name, sc, a, b, token, after=()):
    def body(sc_ref, a_ref, b_ref, out):
        out[...] = added(a_ref, b_ref)

    out = [pltpu.VMEM(a.shape, BF)]
    (out,), token = small_call(name, body, sc, [a, b], out, token, after=after)
    return out, token


def stack_pair(name, sc, a, b, token, after=()):
    def body(sc_ref, a_ref, b_ref, out):
        out[0] = a_ref[...]
        out[1] = b_ref[...]

    out = [pltpu.VMEM((2,) + a.shape, BF)]
    (out,), token = small_call(name, body, sc, [a, b], out, token, after=after)
    return out, token


def unpack(name, sc, plan, parts, out_shapes, token, old=(), small=None, after=()):
    n_parts, n_old = len(parts), len(old)
    width = parts[0].shape[-1]
    total = sum(8 * rows for _, rows, _, _, _ in plan)
    outs = list(old) + [jax.ShapeDtypeStruct(shape, F32) for shape in out_shapes]
    hbm_outs = [jax.ShapeDtypeStruct(v.shape, v.dtype) for v in outs]
    small_outs = []
    if small is not None:
        small_outs = [
            jax.ShapeDtypeStruct(shape, F32)
            for shape in ((1, 2, width), (1, 2, width), (1, small[1] * width), (1, width))
        ]
    n_copies = 8 * len(plan)

    def body(sc_ref, *refs):
        refs = list(refs)
        part_refs = [refs.pop(0) for _ in range(n_parts)]
        for _ in range(n_old):
            refs.pop(0)
        small_refs = [refs.pop(0) for _ in small_outs]
        out_refs = [refs.pop(0) for _ in outs]
        stage, sems = refs
        position = lax.axis_index(DP)
        core, y, z = position % 2, (position // 2) % 2, (position // 4) % 2
        copies = []

        def start(src, dst):
            copy = pltpu.make_async_copy(src, dst, sems.at[len(copies)])
            copy.start()
            copies.append(copy)

        done = 0
        for row, rows, out, out_row, col in plan:
            for place in range(8):
                c = lax.bitwise_xor(core, place // 4)
                first, second = (place // 2) % 2, place % 2
                along_y = jnp.where(c == 0, first, second)
                along_z = jnp.where(c == 0, second, first)
                eighth = (
                    4 * c + 2 * lax.bitwise_xor(along_y, y) + lax.bitwise_xor(along_z, z)
                )
                part = part_refs[place // 2].at[place % 2]
                target = pl.multiple_of(out_row + eighth * rows, rows)
                stage[done : done + rows, :] = part[row : row + rows, :].astype(F32)
                start(
                    stage.at[done : done + rows],
                    out_refs[out].at[pl.ds(target, rows), col : col + width],
                )
                done += rows
                if small is not None and row == plan[-1][0]:

                    @pl.when(eighth == 0)
                    def _(part=part):
                        at, n_up = small
                        rows_ref = part[at : at + SMALL_ROWS, :].astype(F32)
                        gains, biases, b_up, b_down = small_refs
                        for i in range(2):
                            gains[0, i : i + 1, :] = rows_ref[2 * i : 2 * i + 1, :]
                            biases[0, i : i + 1, :] = rows_ref[2 * i + 1 : 2 * i + 2, :]
                        for i in range(n_up):
                            b_up[:, i * width : (i + 1) * width] = rows_ref[4 + i : 5 + i, :]
                        b_down[...] = rows_ref[4 + n_up : 5 + n_up, :]

        for copy in copies:
            copy.wait()

    return small_call(
        name,
        body,
        sc,
        list(parts),
        small_outs,
        token,
        scratch=[pltpu.VMEM((total, width), F32), pltpu.SemaphoreType.DMA((n_copies,))],
        hbm_ins=old,
        hbm_outs=hbm_outs,
        after=after,
        flops=2 * 10**10,
    )


ORDER = (
    "W0", "S", "A0", "W1", "W2", "B0", "A1", "D0", "A2", "B1", "E0", "B2",
    "D1", "F0", "E1", "D2", "F1", "E2", "F2", "U0", "U1", "U2",
)
ARRIVED = {'E1': (('second', 2),), 'U1': (('parts', 2),)}


def per_device(
    inputs,
    lengths,
    cotangent,
    norm_gain,
    layer_norm_biases,
    w_qkv,
    w_out,
    w_up,
    b_up,
    w_down,
    b_down,
):
    slots, seq, width = inputs.shape
    ff = w_up.shape[-1]
    blocks = ff // width
    half = blocks // 2
    n_dp = lax.axis_size(DP)
    sc = lengths
    weights = {"wqkv": w_qkv[0], "wout": w_out[0], "wup": w_up[0], "wdn": w_down[0]}
    vectors = [norm_gain[0], layer_norm_biases[0], b_up, b_down]

    held, recvs = None, {}

    def run_step(step, held, token):
        held, out, token = pipeline_step(
            step, sc, vectors, weights, inputs, cotangent, recvs.get(step - 2), held, token
        )
        if out is not None:
            recvs[step] = lax.ppermute(out, SECTION, [(0, 1), (1, 0)])
        return held, token

    token = None
    for step in range(2 * slots - 1):
        held, token = run_step(step, held, token)
    late = [recvs[k + 2] for k in range(slots)]

    keep, got_core, got_near, got_first, near, got_second = {}, {}, {}, {}, {}, {}
    total, got_far, own, got_own, got_back, got_parts = {}, {}, {}, {}, {}, {}
    eighth = width // 8
    down = [(0, None, b * width, 0) for b in range(blocks)]
    up = [(0, 1, 0, b * width) for b in range(blocks)]
    sums = {}
    arriving = {"core": got_core, "first": got_first, "second": got_second, "far": got_far}
    arriving.update(near=got_near, own=got_own, back=got_back, parts=got_parts)
    for op in ORDER:
        kind, c = op[0], int(op[1:] or 0)
        after = [arriving[which][chunk] for which, chunk in ARRIVED.get(op, ())]
        after = [v[0] if isinstance(v, list) else v for v in after]
        if kind == "S":
            held, token = run_step(2 * slots - 1, held, token)
        elif kind == "W":
            if c == 0:
                sources = [held["a"], held["cotangent"]]
                out, token = weight_gradients(
                    "w_down_grad", sc, down, sources, token, recvs=late, sums_of=[0], after=after
                )
            elif c == 1:
                sources = [held["n2"], held["gu"]]
                out, token = weight_gradients(
                    "w_up_grad",
                    sc,
                    up,
                    sources,
                    token,
                    sums_of=list(range(blocks)),
                    saved=[held["outputs"], held["grads"]],
                    after=after,
                )
                outputs, grads = out[4:]
            else:
                out, token = weight_gradients(
                    "w_attn_grad",
                    sc,
                    [(0, 1, 0, 0)] + [(2, 3, 0, b * width) for b in range(3)],
                    [held[k] for k in ("o", "grb", "n1", "gqkv")],
                    token,
                    small=[held["small"], sums[1], sums[0]],
                    after=after,
                )
            keep[c] = out[0]
            got_core[c] = exchange(out[2], other_core)
            got_near[c] = exchange(out[1], other_core)
            sums[c] = out[3] if len(out) > 3 else None
        elif kind == "A":
            other, token = after_cores(c, sc, keep[c], got_core[c], token, after)
            got_first[c] = exchange(other, first_way)
        elif kind == "B":
            (near[c], other), token = after_first(
                c, sc, keep[c], got_near[c], got_first[c], token, after
            )
            got_second[c] = exchange(other, second_way)
        elif kind == "D":
            total[c], token = add_pair(
                f"second_{c}", sc, near[c], got_second[c], token, after
            )
            got_far[c] = exchange(total[c], lambda i: i ^ 8)
        elif kind == "E":
            value, token = add_pair(f"far_{c}", sc, total[c], got_far[c], token, after)
            bit = 16
            while bit < n_dp:
                other = exchange(value, lambda i, bit=bit: i ^ bit)
                value, token = add_pair(f"bit_{bit}_{c}", sc, value, other, token)
                bit *= 2
            total[c] = value
            got_own[c] = exchange(value, second_way)
        elif kind == "F":
            own[c], token = stack_pair(f"pair_{c}", sc, total[c], got_own[c], token, after)
            got_back[c] = exchange(own[c], first_way)
            got_parts[c] = [exchange(own[c], other_core), exchange(got_back[c], other_core)]
        else:
            parts = [own[c], got_back[c]] + got_parts[c]
            if c == 0:
                plan = [(b * eighth, eighth, 0, b * width, 0) for b in range(blocks)]
                (grad_wdown,), token = unpack(
                    "unpack_down", sc, plan, parts, [(ff, width)], token, after=after
                )
            elif c == 1:
                plan = [(b * eighth, eighth, 0, 0, b * width) for b in range(blocks)]
                (grad_wup,), token = unpack(
                    "unpack_up", sc, plan, parts, [(width, ff)], token, after=after
                )
            else:
                plan = [(0, eighth, 0, 0, 0)]
                plan += [((1 + b) * eighth, eighth, 1, 0, b * width) for b in range(3)]
                (gains, biases, grad_bup, grad_bdown, grad_wout, grad_wqkv), token = unpack(
                    "unpack_attn",
                    sc,
                    plan,
                    parts,
                    [(width, width), (width, 3 * width)],
                    token,
                    small=(4 * eighth, blocks),
                    after=after,
                )
    return (
        outputs[None],
        grads[None],
        gains,
        biases,
        grad_wqkv[None],
        grad_wout[None],
        grad_wup[None],
        grad_bup,
        grad_wdown[None],
        grad_bdown,
    )


def solution(mesh):
    placed = (
        P(DP, None, None),
        P(DP),
        P(DP, None, None),
        P(SECTION, None, None),
        P(SECTION, None, None),
        P(SECTION, None, None),
        P(SECTION, None, None),
        P(SECTION, None, None),
        P(SECTION, None),
        P(SECTION, None, None),
        P(SECTION, None),
    )
    return jax.shard_map(
        per_device,
        mesh=mesh,
        in_specs=placed,
        out_specs=(
            P(SECTION, DP, None, None),
            P(SECTION, DP, None, None),
            P(SECTION, None, None),
            P(SECTION, None, None),
            P(SECTION, None, None),
            P(SECTION, None, None),
            P(SECTION, None, None),
            P(SECTION, None),
            P(SECTION, None, None),
            P(SECTION, None),
        ),
        check_vma=False,
    )
```

```python
import functools

import jax
import jax.numpy as jnp
from jax import lax
from jax.experimental import pallas as pl
from jax.experimental.pallas import tpu as pltpu
from jax.sharding import PartitionSpec as P

SECTION, DP = "section", "dp"
BF = jnp.bfloat16
F32 = jnp.float32
HEAD = 64
GROUP = 4
EPS = 1e-05
GELU_C = 0.7978845608028654
GELU_K = 0.044715
STEP_VMEM = 10 * 2**20
WIDTH = 512


def dot(a, b):
    return lax.dot_general(a, b, (((1,), (0,)), ((), ())), preferred_element_type=F32)


def dot_t(a, b):
    return lax.dot_general(a, b, (((1,), (1,)), ((), ())), preferred_element_type=F32)


def t_dot(a, b):
    return lax.dot_general(a, b, (((0,), (0,)), ((), ())), preferred_element_type=F32)


def norm_parts(stream):
    mean = jnp.mean(stream, -1, keepdims=True)
    centred = stream - mean
    rstd = lax.rsqrt(jnp.mean(centred * centred, -1, keepdims=True) + EPS)
    return centred * rstd, rstd


def norm_back(hat, rstd, gain, grad):
    scaled = grad * gain
    a = jnp.mean(scaled, -1, keepdims=True)
    b = jnp.mean(scaled * hat, -1, keepdims=True)
    return rstd * (scaled - a - hat * b)


def gelu_and_slope(u):
    u = u.astype(BF)
    w = BF(GELU_C) + BF(GELU_C * GELU_K) * (u * u)
    t = BF(0.5) * jnp.tanh(u * w)
    half = BF(0.5) + t
    a = u * half
    return a, half + (a * (BF(0.5) - t)) * (BF(6.0) * w - BF(4.0 * GELU_C))


def head_masks(rows, axis):
    shape = (rows, GROUP * HEAD) if axis == 1 else (GROUP * HEAD, rows)
    lane = lax.broadcasted_iota(jnp.int32, shape, axis)
    return [(lane >= h * HEAD) & (lane < (h + 1) * HEAD) for h in range(GROUP)]


def head_parts(qkv, width):
    gw = GROUP * HEAD
    groups = range(width // gw)
    parts = [
        [qkv[:, j * width + g * gw : j * width + (g + 1) * gw] for g in groups] for j in range(3)
    ]
    parts[0] = [m * BF(HEAD**-0.5) for m in parts[0]]
    return [(g, h) for g in groups for h in range(GROUP)], parts


def layer_forward(x, limit, vec, s, wait):
    seq, width = x.shape
    ff = s["wup"].shape[1]
    gw = GROUP * HEAD
    hat, _ = norm_parts(x)
    n1 = (hat * vec[0:1, 0:width] + vec[0:1, width : 2 * width]).astype(BF)
    s["n1"][...] = n1
    wait("wqkv")
    s["qkv"][...] = dot(n1, s["wqkv"][...]).astype(BF)
    lane_masks = head_masks(seq, 1)
    key_bias = jnp.where(lax.broadcasted_iota(jnp.int32, (1, seq), 1) < limit, 0.0, -1e30)
    heads, (q, k, v) = head_parts(s["qkv"], width)
    zero = jnp.zeros_like(q[0])
    mixed = [jnp.zeros((seq, gw), F32) for _ in q]

    def scores_of(g, h):
        return dot_t(jnp.where(lane_masks[h], q[g], zero), k[g]) + key_bias

    def softmax_of(g, h, scores):
        e = jnp.exp(scores - jnp.max(scores, 1, keepdims=True))
        p = (e * (1.0 / jnp.sum(e, 1, keepdims=True))).astype(BF)
        s["pt"][g, :, h * seq : (h + 1) * seq] = p
        return p

    def mix(g, h, p):
        mixed[g] = jnp.where(lane_masks[h], dot(p, v[g]), mixed[g])

    scores, p = scores_of(*heads[0]), None
    for i, head in enumerate(heads):
        later = scores_of(*heads[i + 1]) if i + 1 < len(heads) else None
        last, p = p, softmax_of(*head, scores)
        if i > 0:
            mix(*heads[i - 1], last)
        scores = later
    mix(*heads[-1], p)
    for g in range(len(q)):
        s["o"][:, g * gw : (g + 1) * gw] = mixed[g].astype(BF)
    wait("wout")
    r = x + dot(s["o"][...], s["wout"][...])
    s["r"][...] = r
    hat, _ = norm_parts(r)
    n2 = (hat * vec[0:1, 2 * width : 3 * width] + vec[0:1, 3 * width : 4 * width]).astype(BF)
    s["n2"][...] = n2
    wait("wup")
    for j in range(ff // width):
        cols = slice(j * width, (j + 1) * width)
        a, slope = gelu_and_slope(dot(n2, s["wup"][:, cols]) + vec[1:2, cols])
        s["a"][:, cols] = a
        s["d"][:, cols] = slope
    wait("wdn")
    y = s["r"][...] + vec[2:3, 0:width] + dot(s["a"][...], s["wdn"][...])
    return y.astype(BF)


def layer_backward(x, gy, vec, s, started):
    seq, width = x.shape
    ff = s["wup"].shape[1]
    gw = GROUP * HEAD
    gyf = gy.astype(F32)
    if started:
        s["gu"][...] = s["gu"][...] * s["d"][...]
    else:
        for j in range(ff // width):
            cols = slice(j * width, (j + 1) * width)
            gu = dot_t(gy, s["wdn"][cols, :]) * s["d"][:, cols].astype(F32)
            s["gu"][:, cols] = gu.astype(BF)
    acc = dot_t(s["gu"][...], s["wup"][...])
    hat, rstd = norm_parts(s["r"][...])
    s["small"][0:1, 2 * width : 3 * width] = jnp.sum(acc * hat, 0, keepdims=True)
    s["small"][0:1, 3 * width : 4 * width] = jnp.sum(acc, 0, keepdims=True)
    gr = gyf + norm_back(hat, rstd, vec[0:1, 2 * width : 3 * width], acc)
    grb = gr.astype(BF)
    s["grb"][...] = grb
    s["r"][...] = gr
    s["go"][...] = dot_t(grb, s["wout"][...]).astype(BF)
    lane_masks = head_masks(seq, 1)
    row_masks = head_masks(seq, 0)
    heads, (q, k, v) = head_parts(s["qkv"], width)
    groups = range(len(q))
    go = [s["go"][:, g * gw : (g + 1) * gw] for g in groups]
    q_t, go_t = [m.T for m in q], [m.T for m in go]
    zero = jnp.zeros_like(q[0])
    gq = [jnp.zeros((seq, gw), F32) for _ in groups]
    gk_t = [jnp.zeros((gw, seq), F32) for _ in groups]
    gv_t = [jnp.zeros((gw, seq), F32) for _ in groups]

    def probs(g, h):
        return s["pt"][g, :, h * seq : (h + 1) * seq]

    def prob_gradient(g, h):
        return dot_t(jnp.where(lane_masks[h], go[g], zero), v[g])

    def score_gradient(g, h, gp):
        p = probs(g, h).astype(F32)
        return (p * (gp - jnp.sum(gp * p, 1, keepdims=True))).astype(BF)

    def spread(g, h, gs):
        gq[g] = jnp.where(lane_masks[h], dot(gs, k[g]), gq[g])
        gk_t[g] = jnp.where(row_masks[h], dot(q_t[g], gs), gk_t[g])

    gp, gs = prob_gradient(*heads[0]), None
    for i, (g, h) in enumerate(heads):
        later = prob_gradient(*heads[i + 1]) if i + 1 < len(heads) else None
        gv_t[g] = jnp.where(row_masks[h], dot(go_t[g], probs(g, h)), gv_t[g])
        last, gs = gs, score_gradient(g, h, gp)
        if i > 0:
            spread(*heads[i - 1], last)
        gp = later
    spread(*heads[-1], gs)
    for g in groups:
        cols = slice(g * gw, (g + 1) * gw)
        for part, value in enumerate((gq[g] * HEAD**-0.5, gk_t[g].T, gv_t[g].T)):
            s["gqkv"][:, part * width + g * gw : part * width + (g + 1) * gw] = value.astype(BF)
    gn = dot_t(s["gqkv"][...], s["wqkv"][...])
    hat, rstd = norm_parts(x)
    s["small"][0:1, 0:width] = jnp.sum(gn * hat, 0, keepdims=True)
    s["small"][0:1, width : 2 * width] = jnp.sum(gn, 0, keepdims=True)
    return (s["r"][...] + norm_back(hat, rstd, vec[0:1, 0:width], gn)).astype(BF)


WEIGHTS = ("wqkv", "wout", "wup", "wdn")
LOADED = WEIGHTS + ("inputs", "cotangent")
VECTORS = ("gains", "biases", "b_up", "b_down")
STORES = (
    ("qkv", "pt", "r", "d")
    + ("n1", "n2", "o", "a")
    + ("gu", "grb", "gqkv", "small")
    + ("outputs", "grads")
)
VMEM = pl.BlockSpec(memory_space=pltpu.VMEM)
SMEM = pl.BlockSpec(memory_space=pltpu.SMEM)
HBM = pl.BlockSpec(memory_space=pltpu.HBM)


def in_vmem(value):
    return pltpu.with_memory_space_constraint(value, pltpu.VMEM)


def shapes_of(seq, width, ff):
    gw = GROUP * HEAD
    return {
        "qkv": ((seq, 3 * width), BF),
        "pt": ((width // gw, seq, GROUP * seq), BF),
        "r": ((seq, width), F32),
        "d": ((seq, ff), BF),
        "n1": ((seq, width), BF),
        "n2": ((seq, width), BF),
        "o": ((seq, width), BF),
        "a": ((seq, ff), BF),
        "gu": ((seq, ff), BF),
        "grb": ((seq, width), BF),
        "gqkv": ((seq, 3 * width), BF),
        "small": ((8, 4 * width), F32),
        "outputs": ((seq, width), BF),
        "grads": ((seq, width), BF),
    }


def step_body(step, slots, names, *refs):
    ref = dict(zip(names, refs))
    sc = ref["sc"]
    first = lax.axis_index(SECTION) == 0
    second = jnp.logical_not(first)
    vec = ref["vec"]

    def view(slot):
        s = {k: ref["held_" + k].at[slot] for k in STORES}
        for k in WEIGHTS + ("go",):
            if k in ref:
                s[k] = ref[k]
        return s

    def ready(name):
        return None

    def row_gradient(slot):
        gy = ref["cotangent"][slot]
        live = lax.broadcasted_iota(jnp.int32, gy.shape, 0) < sc[slot]
        return jnp.where(live, gy, jnp.zeros_like(gy))

    def start_backward(slot):
        ref["held_gu"][slot] = dot_t(row_gradient(slot), ref["wdn"][...]).astype(BF)

    if step == 0:
        sems = ref["sems"]
        copies = {
            k: pltpu.make_async_copy(ref["hbm_" + k], ref[k], sems.at[i])
            for i, k in enumerate(LOADED)
        }
        more = [(ref["hbm_inputs"].at[0], ref["x"]), (ref["sc"], ref["lengths"])]
        more += [(ref["hbm_" + k], ref["v_" + k]) for k in VECTORS]
        more = [
            pltpu.make_async_copy(src, dst, sems.at[len(LOADED) + i])
            for i, (src, dst) in enumerate(more)
        ]
        for copy in more:
            copy.start()
        for k in LOADED:
            copies[k].start()
        for copy in more:
            copy.wait()
        width = ref["x"].shape[1]
        for i in range(2):
            for j, name in enumerate(("gains", "biases")):
                at = (2 * i + j) * width
                vec[0:1, at : at + width] = ref["v_" + name][i : i + 1, :].astype(F32)
        vec[1:2, :] = ref["v_b_up"][...].astype(F32)
        vec[2:3, 0:width] = ref["v_b_down"][...].astype(F32)
        sc = ref["lengths"]

        @pl.when(first)
        def _():
            s = view(0)
            y = layer_forward(
                ref["x"][...].astype(F32),
                jnp.maximum(sc[0], 1),
                vec,
                s,
                lambda name: copies[name].wait(),
            )
            s["outputs"][...] = y
            ref["send"][...] = y

        @pl.when(second)
        def _():
            for k in reversed(WEIGHTS):
                copies[k].wait()

        copies["inputs"].wait()
        copies["cotangent"].wait()

        @pl.when(second)
        def _():
            for slot in range(slots // 2):
                start_backward(slot)

        return

    if step >= slots and "recv" in ref:

        @pl.when(first)
        def _():
            slot = step - slots
            s = view(slot)
            s["grads"][...] = layer_backward(
                ref["inputs"][slot].astype(F32), ref["recv"][...], vec, s, False
            )

    if step == 1:

        @pl.when(second)
        def _():
            for slot in range(slots // 2, slots):
                start_backward(slot)

    if step < slots:

        @pl.when(first)
        def _():
            s = view(step)
            y = layer_forward(
                ref["inputs"][step].astype(F32), jnp.maximum(sc[step], 1), vec, s, ready
            )
            s["outputs"][...] = y
            ref["send"][...] = y

    if "recv" in ref and step < slots + 2:

        @pl.when(jnp.logical_not(first))
        def _():
            slot = step - 2
            s = view(slot)
            s["outputs"][...] = layer_forward(
                ref["recv"][...].astype(F32), jnp.maximum(sc[slot], 1), vec, s, ready
            )
            gx = layer_backward(ref["recv"][...].astype(F32), row_gradient(slot), vec, s, True)
            s["grads"][...] = gx
            ref["send"][...] = gx


def pipeline_step(step, sc, vectors, weights, inputs, cotangent, recv, held, token):
    slots, seq, width = inputs.shape
    ff = weights["wup"].shape[1]
    shapes = shapes_of(seq, width, ff)
    names, args, specs = [], [], []
    out_names, out_shape, aliases = [], [], {}

    def give(name, value, spec):
        names.append(name)
        args.append(value)
        specs.append(spec)

    give("sc", sc, HBM if step == 0 else SMEM)
    for name in STORES:
        shape, kind = shapes[name]
        out_names.append("held_" + name)
        out_shape.append(pltpu.VMEM((slots,) + shape, kind))
    if step == 0:
        for name, value in zip(VECTORS, vectors):
            give("hbm_" + name, pltpu.with_memory_space_constraint(value, pltpu.HBM), HBM)
        out_names.append("vec")
        out_shape.append(pltpu.VMEM((8, 4 * width), F32))
        sources = dict(weights, inputs=inputs, cotangent=cotangent)
        for name in LOADED:
            value = pltpu.with_memory_space_constraint(sources[name], pltpu.HBM)
            give("hbm_" + name, value, HBM)
            out_names.append(name)
            out_shape.append(pltpu.VMEM(value.shape, BF))
    else:
        for name in LOADED + ("vec",):
            give(name, in_vmem(held[name]), VMEM)
        give("token", in_vmem(token), VMEM)
        if recv is not None:
            give("recv", in_vmem(recv), VMEM)
        for i, name in enumerate(STORES):
            aliases[len(args)] = i
            give("in_" + name, in_vmem(held[name]), VMEM)
    out_names.append("token_out")
    out_shape.append(pltpu.VMEM((8, 128), F32))
    sends = step < slots + 2
    if sends:
        out_names.append("send")
        out_shape.append(pltpu.VMEM((seq, width), BF))
    scratch = {}
    if step == 0:
        scratch["x"] = pltpu.VMEM((seq, width), BF)
        scratch["lengths"] = pltpu.SMEM(sc.shape, jnp.int32)
        for name, value in zip(VECTORS, vectors):
            scratch["v_" + name] = pltpu.VMEM(value.shape, BF)
        scratch["sems"] = pltpu.SemaphoreType.DMA((len(LOADED) + 2 + len(VECTORS),))
    if step >= 2:
        scratch["go"] = pltpu.VMEM((seq, width), BF)
    out = pl.pallas_call(
        functools.partial(step_body, step, slots, names + out_names + list(scratch)),
        in_specs=specs,
        out_specs=[VMEM] * len(out_shape),
        out_shape=out_shape,
        scratch_shapes=list(scratch.values()),
        input_output_aliases=aliases,
        compiler_params=pltpu.CompilerParams(vmem_limit_bytes=STEP_VMEM),
        cost_estimate=pl.CostEstimate(
            flops=4 * seq * (width * 4 * width + 2 * width * ff),
            bytes_accessed=2**20,
            transcendentals=0,
        ),
        name=f"step_{step}",
    )(*args)
    result = dict(zip(out_names, out))
    new = {name: result["held_" + name] for name in STORES}
    for name in LOADED + ("vec",):
        new[name] = result[name] if step == 0 else held[name]
    return new, result.get("send"), result["token_out"]


def small_call(
    name, body, sc, ins, outs, token, scratch=(), hbm_ins=(), hbm_outs=(), after=(), flops=0
):
    n_in, n_hbm, n_out = len(ins), len(hbm_ins), len(outs) + len(hbm_outs)
    skip = 1 + len(after)

    def wrapped(sc_ref, *refs):
        refs = refs[skip:]
        at = n_in + n_hbm
        body(sc_ref, *refs[:at], *refs[at : at + n_out], *refs[at + n_out + 1 :])

    first_hbm = 1 + skip + n_in
    out = pl.pallas_call(
        wrapped,
        in_specs=[SMEM] + [VMEM] * (skip + n_in) + [HBM] * n_hbm,
        out_specs=[VMEM] * len(outs) + [HBM] * len(hbm_outs) + [VMEM],
        out_shape=list(outs) + list(hbm_outs) + [pltpu.VMEM((8, 128), F32)],
        scratch_shapes=list(scratch),
        input_output_aliases={first_hbm + i: len(outs) + i for i in range(n_hbm)},
        compiler_params=pltpu.CompilerParams(vmem_limit_bytes=STEP_VMEM),
        cost_estimate=pl.CostEstimate(flops=flops, bytes_accessed=0, transcendentals=0),
        name=name,
    )(
        sc,
        in_vmem(token),
        *[in_vmem(v) for v in after],
        *[in_vmem(v) for v in ins],
        *[pltpu.with_memory_space_constraint(v, pltpu.HBM) for v in hbm_ins],
    )
    return out[:-1], out[-1]


def place_eighths(places, block_row, block):
    keep, near, away = places
    rows = block.shape[0] // 8
    place = lax.axis_index(DP)
    core, y, z = place % 2, (place // 2) % 2, (place // 4) % 2
    for mine, c in ((True, core), (False, 1 - core)):
        for at in range(4):
            first, second = at // 2, at % 2
            target, to = (keep, at) if mine else (away if first else near, second)
            along_y = jnp.where(c == 0, first, second)
            along_z = jnp.where(c == 0, second, first)
            eighth = 4 * c + 2 * lax.bitwise_xor(along_y, y) + lax.bitwise_xor(along_z, z)
            source = pl.multiple_of(eighth * rows, rows)
            target[to, block_row : block_row + rows, :] = block[pl.ds(source, rows), :]


def chunk_shapes(blocks, width, extra=0):
    rows = blocks * width // 8 + extra
    return [pltpu.VMEM((n, rows, width), BF) for n in (4, 2, 2)]


def weight_gradients(
    name, sc, jobs, sources, token, recvs=None, sums_of=(), small=None, saved=(), after=()
):
    slots, seq, width = sources[-1].shape[0], sources[-1].shape[1], WIDTH
    n_src = len(sources)
    ins = list(sources) + list(recvs or []) + list(small or []) + list(saved)
    outs = chunk_shapes(len(jobs), width, SMALL_ROWS if small else 0)
    scratch = [pltpu.VMEM((len(jobs), width, width), BF)]
    if recvs:
        scratch.append(pltpu.VMEM((slots * seq, width), BF))
    if small:
        scratch.append(pltpu.VMEM((8 * SMALL_ROWS, width), F32))
        scratch.append(pltpu.VMEM((8 * SMALL_ROWS, width), BF))
    if sums_of:
        outs.append(pltpu.VMEM((8, len(sums_of) * width), F32))

    def body(sc_ref, *refs):
        refs = list(refs)
        src = [refs.pop(0) for _ in range(n_src)]
        recv_refs = [refs.pop(0) for _ in recvs or []]
        small_refs = [refs.pop(0) for _ in small or []]
        saved_refs = [refs.pop(0) for _ in saved]
        places = [refs.pop(0) for _ in range(3)]
        sums = refs.pop(0) if sums_of else None
        saved_outs = [refs.pop(0) for _ in saved]
        if saved:
            sems = refs.pop()
            copies = [
                pltpu.make_async_copy(src, dst, sems.at[i])
                for i, (src, dst) in enumerate(zip(saved_refs, saved_outs))
            ]
            for copy in copies:
                copy.start()
        blocks = refs.pop(0)
        gm = refs.pop(0) if recvs else None
        if recvs:
            first = lax.axis_index(SECTION) == 0

            @pl.when(first)
            def _():
                for k in range(slots):
                    gm[k * seq : (k + 1) * seq, :] = recv_refs[k][...]

            @pl.when(jnp.logical_not(first))
            def _():
                for k in range(slots):
                    live = lax.broadcasted_iota(jnp.int32, (seq, width), 0) < sc_ref[k]
                    gm[k * seq : (k + 1) * seq, :] = jnp.where(
                        live, src[-1][k], jnp.zeros((seq, width), BF)
                    )

        def rows(ref, col):
            return ref[:, :, col : col + width].reshape(slots * seq, width)

        for n, (i, j, left_col, right_col) in enumerate(jobs):
            right = gm[...] if j is None else rows(src[j], right_col)
            blocks[n] = t_dot(rows(src[i], left_col), right).astype(BF)
            if n in sums_of:
                at = sums_of.index(n) * width
                sums[0:1, at : at + width] = jnp.sum(right.astype(F32), 0, keepdims=True)
            if n > 0:
                place_eighths(places, (n - 1) * (width // 8), blocks.at[n - 1])
        place_eighths(places, (len(jobs) - 1) * (width // 8), blocks.at[len(jobs) - 1])
        if small:
            block = refs.pop(0)
            block[...] = jnp.zeros_like(block)
            norms = jnp.sum(small_refs[0][:, 0:1, :], 0)
            row = 0
            for value in [norms] + [r[0:1, :] for r in small_refs[1:]]:
                for i in range(value.shape[1] // width):
                    block[row : row + 1, :] = value[:, i * width : (i + 1) * width]
                    row += 1
            rounded = refs.pop(0)
            rounded[...] = block[...].astype(BF)
            place_eighths(places, len(jobs) * (width // 8), rounded)
        if saved:
            for copy in copies:
                copy.wait()

    if saved:
        scratch.append(pltpu.SemaphoreType.DMA((len(saved),)))
    hbm_outs = [jax.ShapeDtypeStruct(v.shape, v.dtype) for v in saved]
    return small_call(name, body, sc, ins, outs, token, scratch, hbm_outs=hbm_outs, after=after)


SMALL_ROWS = 16


def added(a, b):
    return (a[...].astype(F32) + b[...].astype(F32)).astype(BF)


def exchange(value, fn):
    n = lax.axis_size(DP)
    return lax.ppermute(value, DP, [(i, fn(i)) for i in range(n)])


def other_core(i):
    return i ^ 1


def first_way(i):
    return i ^ 2 if i % 2 == 0 else i ^ 4


def second_way(i):
    return i ^ 4 if i % 2 == 0 else i ^ 2


def added3(a, b, c):
    return (a[...].astype(F32) + b[...].astype(F32) + c[...].astype(F32)).astype(BF)


def after_cores(c, sc, keep, got, token, after=()):
    def body(sc_ref, keep_ref, got_ref, other):
        for p in range(2):
            other[p] = added(keep_ref.at[2 + p], got_ref.at[p])

    out = [pltpu.VMEM((2,) + keep.shape[1:], BF)]
    (out,), token = small_call(f"cores_{c}", body, sc, [keep, got], out, token, after=after)
    return out, token


def after_first(c, sc, keep, got_near, got, token, after=()):
    def body(sc_ref, keep_ref, core_ref, got_ref, near, other):
        near[...] = added3(keep_ref.at[0], core_ref.at[0], got_ref.at[0])
        other[...] = added3(keep_ref.at[1], core_ref.at[1], got_ref.at[1])

    out = pltpu.VMEM(keep.shape[1:], BF)
    ins = [keep, got_near, got]
    return small_call(f"first_{c}", body, sc, ins, [out, out], token, after=after)


def add_pair(name, sc, a, b, token, after=()):
    def body(sc_ref, a_ref, b_ref, out):
        out[...] = added(a_ref, b_ref)

    out = [pltpu.VMEM(a.shape, BF)]
    (out,), token = small_call(name, body, sc, [a, b], out, token, after=after)
    return out, token


def stack_pair(name, sc, a, b, token, after=()):
    def body(sc_ref, a_ref, b_ref, out):
        out[0] = a_ref[...]
        out[1] = b_ref[...]

    out = [pltpu.VMEM((2,) + a.shape, BF)]
    (out,), token = small_call(name, body, sc, [a, b], out, token, after=after)
    return out, token


def copy_of(name, sc, value, token):
    def body(sc_ref, value_ref, out):
        out[...] = value_ref[...]

    (out,), token = small_call(name, body, sc, [value], [pltpu.VMEM(value.shape, BF)], token)
    return out, token


def unpack(name, sc, plan, parts, out_shapes, token, old=(), small=None, old_small=(), after=()):
    numbers, pairs = list(parts), list(parts.values())
    n_parts, n_old = len(pairs), len(old)
    width = pairs[0].shape[-1]
    total = sum(2 * n_parts * rows for _, rows, _, _, _ in plan)
    outs = list(old) + [jax.ShapeDtypeStruct(shape, F32) for shape in out_shapes]
    hbm_outs = [jax.ShapeDtypeStruct(v.shape, v.dtype) for v in outs]
    small_outs = []
    if small is not None:
        small_outs = [
            jax.ShapeDtypeStruct(shape, F32)
            for shape in ((1, 2, width), (1, 2, width), (1, small[1] * width), (1, width))
        ]
    n_copies = 2 * n_parts * len(plan)

    def body(sc_ref, *refs):
        refs = list(refs)
        part_refs = [refs.pop(0) for _ in range(n_parts)]
        old_small_refs = [refs.pop(0) for _ in old_small]
        for _ in range(n_old):
            refs.pop(0)
        small_refs = [refs.pop(0) for _ in small_outs]
        out_refs = [refs.pop(0) for _ in outs]
        stage, sems = refs
        position = lax.axis_index(DP)
        core, y, z = position % 2, (position // 2) % 2, (position // 4) % 2
        copies = []
        for old_ref, ref in zip(old_small_refs, small_refs):
            ref[...] = old_ref[...]
        done = 0
        for row, rows, out, out_row, col in plan:
            for number, pair in zip(numbers, part_refs):
                for second in range(2):
                    c = lax.bitwise_xor(core, number // 2)
                    first = number % 2
                    along_y = jnp.where(c == 0, first, second)
                    along_z = jnp.where(c == 0, second, first)
                    eighth = (
                        4 * c + 2 * lax.bitwise_xor(along_y, y) + lax.bitwise_xor(along_z, z)
                    )
                    part = pair.at[second]
                    target = pl.multiple_of(out_row + eighth * rows, rows)
                    stage[done : done + rows, :] = part[row : row + rows, :].astype(F32)
                    copy = pltpu.make_async_copy(
                        stage.at[done : done + rows],
                        out_refs[out].at[pl.ds(target, rows), col : col + width],
                        sems.at[len(copies)],
                    )
                    copy.start()
                    copies.append(copy)
                    done += rows
                    if small is not None and row == plan[-1][0]:

                        @pl.when(eighth == 0)
                        def _(part=part):
                            at, n_up = small
                            rows_ref = part[at : at + SMALL_ROWS, :].astype(F32)
                            gains, biases, b_up, b_down = small_refs
                            for i in range(2):
                                gains[0, i : i + 1, :] = rows_ref[2 * i : 2 * i + 1, :]
                                biases[0, i : i + 1, :] = rows_ref[2 * i + 1 : 2 * i + 2, :]
                            for i in range(n_up):
                                b_up[:, i * width : (i + 1) * width] = rows_ref[4 + i : 5 + i, :]
                            b_down[...] = rows_ref[4 + n_up : 5 + n_up, :]

        for copy in copies:
            copy.wait()

    return small_call(
        name,
        body,
        sc,
        pairs + list(old_small),
        small_outs,
        token,
        scratch=[pltpu.VMEM((total, width), F32), pltpu.SemaphoreType.DMA((n_copies,))],
        hbm_ins=old,
        hbm_outs=hbm_outs,
        after=after,
        flops=2 * 10**10,
    )


ORDER = (
    "W0", "S", "A0", "W1", "W2", "B0", "A1", "D0", "A2", "B1", "E0", "B2",
    "D1", "F0", "E1", "D2", "F1", "E2", "F2", "U0", "U1", "U2", "U3",
)
ARRIVED = {'E1': (('second', 2),), 'U1': (('parts', 2),)}


def per_device(
    inputs,
    lengths,
    cotangent,
    norm_gain,
    layer_norm_biases,
    w_qkv,
    w_out,
    w_up,
    b_up,
    w_down,
    b_down,
):
    slots, seq, width = inputs.shape
    ff = w_up.shape[-1]
    blocks = ff // width
    half = blocks // 2
    n_dp = lax.axis_size(DP)
    sc = lengths
    weights = {"wqkv": w_qkv[0], "wout": w_out[0], "wup": w_up[0], "wdn": w_down[0]}
    vectors = [norm_gain[0], layer_norm_biases[0], b_up, b_down]

    held, recvs = None, {}

    def run_step(step, held, token):
        held, out, token = pipeline_step(
            step, sc, vectors, weights, inputs, cotangent, recvs.get(step - 2), held, token
        )
        if out is not None:
            recvs[step] = lax.ppermute(out, SECTION, [(0, 1), (1, 0)])
        return held, token

    token = None
    for step in range(2 * slots - 1):
        held, token = run_step(step, held, token)
    late = [recvs[k + 2] for k in range(slots)]

    keep, got_core, got_near, got_first, near, got_second = {}, {}, {}, {}, {}, {}
    total, got_far, own, got_own, got_back, got_parts = {}, {}, {}, {}, {}, {}
    eighth = width // 8
    down = [(0, None, b * width, 0) for b in range(blocks)]
    up = [(0, 1, 0, b * width) for b in range(blocks)]
    sums = {}
    arriving = {"core": got_core, "first": got_first, "second": got_second, "far": got_far}
    arriving.update(near=got_near, own=got_own, back=got_back, parts=got_parts)
    for op in ORDER:
        kind, c = op[0], int(op[1:] or 0)
        after = [arriving[which][chunk] for which, chunk in ARRIVED.get(op, ())]
        after = [v[0] if isinstance(v, list) else v for v in after]
        if kind == "S":
            held, token = run_step(2 * slots - 1, held, token)
        elif kind == "W":
            if c == 0:
                sources = [held["a"], held["cotangent"]]
                out, token = weight_gradients(
                    "w_down_grad", sc, down, sources, token, recvs=late, sums_of=[0], after=after
                )
            elif c == 1:
                sources = [held["n2"], held["gu"]]
                out, token = weight_gradients(
                    "w_up_grad",
                    sc,
                    up,
                    sources,
                    token,
                    sums_of=list(range(blocks)),
                    saved=[held["outputs"], held["grads"]],
                    after=after,
                )
                outputs, grads = out[4:]
            else:
                out, token = weight_gradients(
                    "w_attn_grad",
                    sc,
                    [(0, 1, 0, 0)] + [(2, 3, 0, b * width) for b in range(3)],
                    [held[k] for k in ("o", "grb", "n1", "gqkv")],
                    token,
                    small=[held["small"], sums[1], sums[0]],
                    after=after,
                )
            keep[c] = out[0]
            got_core[c] = exchange(out[2], other_core)
            got_near[c] = exchange(out[1], other_core)
            sums[c] = out[3] if len(out) > 3 else None
        elif kind == "A":
            other, token = after_cores(c, sc, keep[c], got_core[c], token, after)
            got_first[c] = exchange(other, first_way)
        elif kind == "B":
            (near[c], other), token = after_first(
                c, sc, keep[c], got_near[c], got_first[c], token, after
            )
            got_second[c] = exchange(other, second_way)
        elif kind == "D":
            total[c], token = add_pair(
                f"second_{c}", sc, near[c], got_second[c], token, after
            )
            got_far[c] = exchange(total[c], lambda i: i ^ 8)
        elif kind == "E":
            value, token = add_pair(f"far_{c}", sc, total[c], got_far[c], token, after)
            bit = 16
            while bit < n_dp:
                other = exchange(value, lambda i, bit=bit: i ^ bit)
                value, token = add_pair(f"bit_{bit}_{c}", sc, value, other, token)
                bit *= 2
            total[c] = value
            got_own[c] = exchange(value, second_way)
        elif kind == "F":
            own[c], token = stack_pair(f"pair_{c}", sc, total[c], got_own[c], token, after)
            got_back[c] = exchange(own[c], first_way)
            got_parts[c] = [exchange(own[c], other_core)]
            got_parts[c].append(exchange(got_back[c], other_core) if c < 2 else None)
        else:
            if c == 2:
                got_back[c], token = copy_of("back", sc, got_back[c], token)
                got_parts[c][1] = exchange(got_back[c], other_core)
            plan = []
            parts = {}
            if c < 2:
                parts = dict(enumerate([own[c], got_back[c]] + got_parts[c]))
            if c == 0:
                plan = [(b * eighth, eighth, 0, b * width, 0) for b in range(blocks)]
                (grad_wdown,), token = unpack(
                    "unpack_down", sc, plan, parts, [(ff, width)], token, after=after
                )
            elif c == 1:
                plan = [(b * eighth, eighth, 0, 0, b * width) for b in range(blocks)]
                (grad_wup,), token = unpack(
                    "unpack_up", sc, plan, parts, [(width, ff)], token, after=after
                )
            else:
                plan = [(0, eighth, 0, 0, 0)]
                plan += [((1 + b) * eighth, eighth, 1, 0, b * width) for b in range(3)]
                if c == 2:
                    parts = {0: own[2], 1: got_back[2], 2: got_parts[2][0]}
                    earlier, shapes = {}, [(width, width), (width, 3 * width)]
                else:
                    parts = {3: got_parts[2][1]}
                    earlier, shapes = {"old": last[4:], "old_small": last[:4]}, []
                last, token = unpack(
                    f"unpack_attn_{c - 2}",
                    sc,
                    plan,
                    parts,
                    shapes,
                    token,
                    small=(4 * eighth, blocks),
                    after=after,
                    **earlier,
                )
    gains, biases, grad_bup, grad_bdown, grad_wout, grad_wqkv = last
    return (
        outputs[None],
        grads[None],
        gains,
        biases,
        grad_wqkv[None],
        grad_wout[None],
        grad_wup[None],
        grad_bup,
        grad_wdown[None],
        grad_bdown,
    )


def solution(mesh):
    placed = (
        P(DP, None, None),
        P(DP),
        P(DP, None, None),
        P(SECTION, None, None),
        P(SECTION, None, None),
        P(SECTION, None, None),
        P(SECTION, None, None),
        P(SECTION, None, None),
        P(SECTION, None),
        P(SECTION, None, None),
        P(SECTION, None),
    )
    return jax.shard_map(
        per_device,
        mesh=mesh,
        in_specs=placed,
        out_specs=(
            P(SECTION, DP, None, None),
            P(SECTION, DP, None, None),
            P(SECTION, None, None),
            P(SECTION, None, None),
            P(SECTION, None, None),
            P(SECTION, None, None),
            P(SECTION, None, None),
            P(SECTION, None),
            P(SECTION, None, None),
            P(SECTION, None),
        ),
        check_vma=False,
    )
```
